128 devices in a mesh: member: 4 (over x), group: 32 (over y, z, core).
Axes of the slice: x: 4, y: 4, z: 4, core: 2. Of those that a mesh axis runs over, the one named last changes fastest.
Arguments:
- agg_one: bfloat16 [65536, 768], P(('member', 'group')), may hold values from -6 to 6
- agg_two: bfloat16 [65536, 768], P(('member', 'group')), may hold values from -6 to 6
- grad_out: bfloat16 [65536, 768], P(('member', 'group')), may hold values from -6 to 6
- hop_one_weight: bfloat16 [768, 768], replicated, may hold values from -0.21875 to 0.21875
- hop_two_weight: bfloat16 [768, 768], replicated, may hold values from -0.21875 to 0.21875
- block_values: bfloat16 [6144, 256, 256], P(('member', 'group')), may hold values from 0 to 0.046875
- src_slot: int32 [128, 48], P(('member', 'group')), may hold values from 0 to 37, as said below
- dst_block: int32 [128, 48], P(('member', 'group')), may hold values from 0 to 1
- block_count: int32 [128], P(('member', 'group')), may hold values from 33 to 48, as said below
- send_member: int32 [128, 4, 1], P(('member', 'group')), may hold values from 0 to 1, as said below
- send_group: int32 [128, 32], P(('member', 'group')), may hold values from 0 to 1, as said below
Outputs:
- grad_emb: bfloat16 [65536, 768], P(('member', 'group'))
- grad_w_one: float32 [768, 768], replicated
- grad_w_two: float32 [768, 768], replicated
The draws below stay inside these ranges and needn't reach their ends.
Inputs may be any that keep to these rules, and one draw needn't show every extreme that they name: `send_member`: for device d, entry [d, p, 0] is the label block of d, counted within d, sent to the device of member index p in d's group; one for every p. `send_group`: entry [d, h] is the label block of d, counted within d, sent to the device of group h with d's member index; one for every h. The first block_count[d] slots of device d are live, the rest hold 0 in src_slot and dst_block and are not read; some device has all 48 slots live. `src_slot`: encodes the source block as in the reference program. For device d of group g, slot j < 32 - 1 holds 2 + 4 + ((g + 1 + j) % 32); every later slot holds a value under 2 + 4.
All inputs are finite; a program needn't handle non-finite values.
Results may differ from the reference program's by a relative error of at most 0.0065.
Values may be sent and summed in bfloat16 or wider, within the bound.
A program may use at most 128 MiB of HBM per device.

```python
import jax
import jax.numpy as jnp
from jax import lax

D = 768
BLK = 256
RB = 2
MCAP = 1
NBS = 48
NRB = 256
LABELS = 65536
N_MEMBER = 4
N_GROUP = 32
DEVICES = 128


def graph_tables(key):
    base = jax.random.fold_in(key, 7001)
    keys = jax.random.split(base, 9)
    scores = jax.random.randint(keys[0], (DEVICES, N_MEMBER, RB), 0, 1 << 20) * RB + jnp.arange(RB, dtype=jnp.int32)
    ordered = jnp.argsort(scores, axis=-1, stable=True)
    send_member = ordered[:, :, :MCAP].astype(jnp.int32)
    send_group = jax.random.randint(keys[1], (DEVICES, N_GROUP), 0, RB).astype(jnp.int32)
    counts = jax.random.randint(keys[2], (DEVICES,), N_GROUP - 1 + RB, NBS + 1)
    full_device = jax.random.randint(keys[3], (), 0, DEVICES)
    counts = jnp.where(jnp.arange(DEVICES, dtype=jnp.int32) == full_device, NBS, counts).astype(jnp.int32)
    kinds = jax.random.randint(keys[4], (DEVICES, NBS), 0, 10)
    local_pick = jax.random.randint(keys[5], (DEVICES, NBS), 0, RB)
    member_pick = jax.random.randint(keys[6], (DEVICES, NBS), 0, N_MEMBER * MCAP)
    own_group = (jnp.arange(DEVICES, dtype=jnp.int32) % N_GROUP)[:, None]
    slot_pos = jnp.arange(NBS, dtype=jnp.int32)[None, :]
    cross_pick = (own_group + 1 + slot_pos) % N_GROUP
    slot_ids = jnp.where(slot_pos < N_GROUP - 1, RB + N_MEMBER * MCAP + cross_pick, jnp.where(kinds < 4, local_pick, RB + member_pick))
    live_mask = slot_pos < counts[:, None]
    slot_ids = jnp.where(live_mask, slot_ids, 0).astype(jnp.int32)
    targets = jnp.where(live_mask, jax.random.randint(keys[8], (DEVICES, NBS), 0, RB), 0).astype(jnp.int32)
    return (send_member, send_group, counts, slot_ids, targets)


def draw_send_member(key, part):
    return graph_tables(key)[0]


def draw_send_group(key, part):
    return graph_tables(key)[1]


def draw_block_count(key, part):
    return graph_tables(key)[2]


def draw_src_slot(key, part):
    return graph_tables(key)[3]


def draw_dst_block(key, part):
    return graph_tables(key)[4]


def block_levels(rng, dims, shards, smallest, top_value):
    def one(dim, blocks):
        heights = jax.random.uniform(jax.random.fold_in(jax.random.fold_in(rng, 6), dim), (blocks,), jnp.float32, smallest / len(shards), top_value / len(shards))
        return jnp.repeat(jnp.exp(heights), dims[dim] // blocks).reshape((-1,) + (1,) * (len(dims) - dim - 1))

    gain = one(*shards[0])
    for cut in shards[1:]:
        gain = gain * one(*cut)
    return gain


def bell_draw(key, shape, spread, limit, cuts=(), kind=jnp.bfloat16):
    level = block_levels(key, shape, cuts, -0.22, 0.18) if cuts else 1.0
    array = jax.random.normal(key, shape, jnp.float32) * spread * level
    return jnp.minimum(jnp.maximum(array, -limit), limit).astype(kind)


def setup_inputs(seed: int = 0) -> dict:
    streams_of = jax.random.split(jax.random.key(seed), 12)
    agg_one = bell_draw(streams_of[0], (LABELS, D), 1.0, 6.0, ((0, 128),))
    agg_two = bell_draw(streams_of[1], (LABELS, D), 1.0, 6.0, ((0, 128),))
    grad_out = bell_draw(streams_of[2], (LABELS, D), 1.0, 6.0, ((0, 128),))
    hop_one_weight = bell_draw(streams_of[3], (D, D), D ** -0.5, 0.21875)
    hop_two_weight = bell_draw(streams_of[4], (D, D), D ** -0.5, 0.21875)
    block_values = jnp.clip(0.046875 * jax.random.uniform(streams_of[5], (DEVICES * NBS, BLK, BLK), jnp.float32) ** block_levels(streams_of[5], (DEVICES * NBS, BLK, BLK), ((0, 128),), -0.2, 0.2), 0.0, 0.046875).astype(jnp.bfloat16)
    src_slot = draw_src_slot(jax.random.fold_in(streams_of[11], 71), 0)
    dst_block = draw_dst_block(jax.random.fold_in(streams_of[11], 71), 0)
    block_count = draw_block_count(jax.random.fold_in(streams_of[11], 71), 0)
    send_member = draw_send_member(jax.random.fold_in(streams_of[11], 71), 0)
    send_group = draw_send_group(jax.random.fold_in(streams_of[11], 71), 0)
    return dict(agg_one=agg_one, agg_two=agg_two, grad_out=grad_out, hop_one_weight=hop_one_weight, hop_two_weight=hop_two_weight, block_values=block_values, src_slot=src_slot, dst_block=dst_block, block_count=block_count, send_member=send_member, send_group=send_group)


def silu_slope(value):
    sig = jax.nn.sigmoid(value)
    return sig * (1.0 + value * (1.0 - sig))


def transposed_aggregate(field, block_values, src_slot, dst_block, block_count, send_member, send_group):
    all_blocks = field.reshape(NRB, BLK, D)

    def one_device(device):
        member_pos = device // N_GROUP
        group_pos = device % N_GROUP
        slot_ids = src_slot[device]
        member_off = jnp.clip(slot_ids - RB, 0, N_MEMBER * MCAP - 1)
        peer_member = member_off // MCAP
        slot_in_peer = member_off % MCAP
        peer_device = peer_member * N_GROUP + group_pos
        member_pick = send_member[peer_device, member_pos, slot_in_peer]
        cross_group = jnp.clip(slot_ids - RB - N_MEMBER * MCAP, 0, N_GROUP - 1)
        cross_device = member_pos * N_GROUP + cross_group
        cross_pick = send_group[cross_device, group_pos]
        source_block = jnp.where(slot_ids < RB, device * RB + slot_ids,
                                 jnp.where(slot_ids < RB + N_MEMBER * MCAP, peer_device * RB + member_pick,
                                           cross_device * RB + cross_pick)).astype(jnp.int32)
        pieces = all_blocks[source_block].astype(jnp.float32)
        block_vals = lax.dynamic_slice_in_dim(block_values, (device * NBS).astype(jnp.int32), NBS, 0).astype(jnp.float32)
        live_mask = jnp.arange(NBS, dtype=jnp.int32) < block_count[device]
        one_hot = ((dst_block[device][:, None] == jnp.arange(RB, dtype=jnp.int32)[None, :]) & live_mask[:, None]).astype(jnp.float32)
        products = jnp.einsum('kab,kad->kbd', block_vals, pieces)
        return jnp.einsum('kr,kbd->rbd', one_hot, products)

    summed = lax.map(one_device, jnp.arange(DEVICES, dtype=jnp.int32))
    return summed.reshape(LABELS, D)


def reference(agg_one, agg_two, grad_out, hop_one_weight, hop_two_weight, block_values, src_slot, dst_block, block_count, send_member, send_group):
    grad_scale = float(LABELS) ** -0.5
    lift_one = jnp.dot(agg_one, hop_one_weight, preferred_element_type=jnp.float32)
    lift_two = jnp.dot(agg_two, hop_two_weight, preferred_element_type=jnp.float32)
    pull_two = (grad_out.astype(jnp.float32) * silu_slope(lift_two)).astype(jnp.bfloat16)
    grad_w_two = jnp.dot(agg_two.T, pull_two, preferred_element_type=jnp.float32) * grad_scale
    back_two = jnp.dot(pull_two, hop_two_weight.T, preferred_element_type=jnp.float32).astype(jnp.bfloat16)
    carry_grad = grad_out.astype(jnp.float32) + transposed_aggregate(back_two, block_values, src_slot, dst_block, block_count, send_member, send_group)
    pull_one = (carry_grad * silu_slope(lift_one)).astype(jnp.bfloat16)
    grad_w_one = jnp.dot(agg_one.T, pull_one, preferred_element_type=jnp.float32) * grad_scale
    back_one = jnp.dot(pull_one, hop_one_weight.T, preferred_element_type=jnp.float32).astype(jnp.bfloat16)
    grad_emb = (carry_grad + transposed_aggregate(back_one, block_values, src_slot, dst_block, block_count, send_member, send_group)).astype(jnp.bfloat16)
    return (grad_emb, grad_w_one, grad_w_two)
```

```python
import functools

import jax
import jax.numpy as jnp
from jax import lax
from jax.experimental import pallas as pl
from jax.experimental.pallas import tpu as pltpu
from jax.sharding import PartitionSpec as P

MESH = pl.DeviceIdType.MESH
SIDE = 4

ARRIVE = (
    (((1, 0, 0), (3, 0, 0), (0, 1, 1), (0, 3, 1)), ()),
    (((1, 0, 1), (3, 0, 1), (0, 1, 0), (0, 3, 0)), ((1, 0), (3, 0), (0, 1), (0, 3))),
    (((2, 0, 0), (0, 2, 1)), ()),
    (((1, 1, 1), (3, 1, 1), (1, 1, 0), (1, 3, 0)), ((1, 1),)),
    (((1, 3, 1), (3, 3, 1), (3, 1, 0), (3, 3, 0)), ((1, 3), (3, 1), (3, 3))),
    (((2, 0, 1), (0, 2, 0)), ((2, 0), (0, 2))),
    (((1, 2, 1), (3, 2, 1), (2, 1, 0), (2, 3, 0)), ()),
    (((2, 1, 1), (1, 2, 0)), ((2, 1), (1, 2))),
    (((2, 3, 1), (3, 2, 0)), ((2, 3), (3, 2))),
    (((2, 2, 1), (2, 2, 0)), ((2, 2),)),
)


def slope(value):
    sig = jax.nn.sigmoid(value)
    return sig * (1.0 + value * (1.0 - sig))


def across(left, right, dims):
    return lax.dot_general(left, right, (dims, ((), ())), preferred_element_type=jnp.float32)


def hop_kernel(
    scale,
    picks, slots, targets, count, lists,
    agg, weight, grad, values_hbm,
    out, gout,
    pool, values, member_out, member_in, pull,
    part, part_core, part_x_out, part_x_in, part_y, part_y_in, part_z, total_y, total,
    values_sem, ring_send, ring_recv, core_send, core_recv, member_send, member_recv,
    pc_send, pc_recv, px_send, px_recv, py_send, py_recv, pz_send, pz_recv,
    ty_send, ty_recv, tx_send, tx_recv, tc_send, tc_recv,
):
    blk = values.shape[1]
    width = weight.shape[0]
    slot_total = values.shape[0]
    half = blk // 2
    m = lax.axis_index("member")
    g = lax.axis_index("group")
    y, z, c = g // (2 * SIDE), (g // 2) % SIDE, g % 2

    def at(dy, dz, other=0):
        core = c if other == 0 else 1 - c
        return (((y + dy) % SIDE) * SIDE + (z + dz) % SIDE) * 2 + core

    partner = {"group": at(0, 0, 1)}

    load_values = pltpu.make_async_copy(values_hbm, values, values_sem)
    load_values.start()

    barrier = pltpu.get_barrier_semaphore()
    for d in range(1, SIDE):
        for peer in ({"group": at(d, 0)}, {"group": at(0, d)}, {"member": (m + d) % SIDE}):
            pl.semaphore_signal(barrier, inc=1, device_id=peer, device_id_type=MESH)
    pl.semaphore_signal(barrier, inc=1, device_id=partner, device_id_type=MESH)
    pl.semaphore_wait(barrier, 3 * (SIDE - 1) + 1)

    def remote(src, dst, send, recv, peer):
        return pltpu.make_async_remote_copy(
            src_ref=src, dst_ref=dst, send_sem=send, recv_sem=recv, device_id=peer, device_id_type=MESH
        )

    def ring(dy, dz, b, axis, way):
        d = dy if axis == 0 else dz
        rows = pl.ds(0, blk) if d != 2 else pl.ds(0 if way == 1 else half, half)
        sdy, sdz = ((dy - way) % SIDE, dz) if axis == 0 else (dy, (dz - way) % SIDE)
        peer = {"group": at(way, 0) if axis == 0 else at(0, way)}
        part_of = 0 if way == 1 else 1
        return remote(
            pool.at[0, sdy * SIDE + sdz, b, rows],
            pool.at[0, dy * SIDE + dz, b, rows],
            ring_send.at[dy * SIDE + dz, b, part_of],
            ring_recv.at[dy * SIDE + dz, b, part_of],
            peer,
        )

    def arrivals(dy, dz, b):
        axis, d = (1, dz) if b == 0 else (0, dy)
        if d == 0:
            axis, d = (0, dy) if b == 0 else (1, dz)
        ways = {1: (1,), 3: (-1,), 2: (1, -1)}[d]
        return [(dy, dz, b, axis, way) for way in ways]

    def to_core(r, b):
        return remote(
            pool.at[0, r, b], pool.at[1, r, b], core_send.at[r, b], core_recv.at[r, b], partner
        )

    sent = []

    def forward(dy, dz, b):
        first, second = (0, 1) if b == 0 else (1, 0)
        pos = (dy, dz)
        moved = []
        d1, d2 = pos[first], pos[second]

        def step(axis, way):
            new = list(pos)
            new[axis] = (new[axis] + way) % SIDE
            return (new[0], new[1], b, axis, way)

        if d2 == 0:
            if d1 == 0:
                moved += [step(first, 1), step(first, -1)]
            elif d1 == 1:
                moved.append(step(first, 1))
            elif d1 == 3:
                moved.append(step(first, -1))
            moved += [step(second, 1), step(second, -1)]
        elif d2 == 1:
            moved.append(step(second, 1))
        elif d2 == 3:
            moved.append(step(second, -1))
        for key in moved:
            copy = ring(*key)
            copy.start()
            sent.append(copy)
        copy = to_core(dy * SIDE + dz, b)
        copy.start()
        sent.append(copy)

    rows_at = min(128, blk)

    for b in range(2):

        @pl.loop(0, blk // rows_at)
        def _(i, b=b):
            inner = pl.ds(pl.multiple_of(i * rows_at, rows_at), rows_at)
            rows = pl.ds(pl.multiple_of(b * blk + i * rows_at, rows_at), rows_at)
            lift = across(agg[rows, :], weight[...], ((1,), (0,)))
            pulled = (grad[rows, :].astype(jnp.float32) * slope(lift)).astype(jnp.bfloat16)
            pull[rows, :] = pulled
            back = across(pulled, weight[...], ((1,), (1,))).astype(jnp.bfloat16)
            pool[0, 0, b, inner, :] = back

        forward(0, 0, b)

    cut = min(256, width)

    @pl.loop(0, width // cut)
    def _(i):
        rows = pl.ds(pl.multiple_of(i * cut, cut), cut)
        part[rows, :] = across(agg[:, rows], pull[...], ((0,), (0,))) * scale

    half_rows, x_rows = width // 2, width // 8
    y_rows = x_rows // SIDE
    mine = pl.ds(pl.multiple_of(c * half_rows, half_rows), half_rows)
    theirs = pl.ds(pl.multiple_of((1 - c) * half_rows, half_rows), half_rows)
    pc = remote(part.at[theirs], part_core, pc_send, pc_recv, partner)
    pc.start()
    sent.append(pc)

    member_copies = []
    for d in range(1, SIDE):
        chosen = lists[(m + d) % SIDE]
        member_out[d - 1] = jnp.where(chosen == 0, pool[0, 0, 0], pool[0, 0, 1])
        copy = remote(
            member_out.at[d - 1], member_in.at[2 + m], member_send.at[d - 1], member_recv.at[d - 1],
            {"member": (m + d) % SIDE},
        )
        copy.start()
        sent.append(copy)
    member_in[0] = pool[0, 0, 0]
    member_in[1] = pool[0, 0, 1]
    member_in[2 + m] = jnp.where(lists[m] == 0, pool[0, 0, 0], pool[0, 0, 1])

    out[...] = grad[...].astype(jnp.float32)
    load_values.wait()

    @pl.loop(0, slot_total)
    def _(k):
        values[k] = values[k].T

    def cols_of(n):
        return pl.ds(pl.multiple_of(n * cut, cut), cut)

    def kept(k, live):
        value = values[k]
        zero = jnp.zeros_like(value)
        where = targets[k]
        return (
            jnp.where(jnp.logical_and(live, where == 0), value, zero),
            jnp.where(jnp.logical_and(live, where == 1), value, zero),
        )

    def sweep(other, sources):
        groups = 2 * SIDE * SIDE

        @pl.loop(0, width // cut)
        def _(n):
            cols = cols_of(n)
            top, low = out[0:blk, cols], out[blk:2 * blk, cols]
            for dy, dz in sources:
                source = at(-dy, -dz, other)
                k = (source - g - 1 + groups) % groups
                r = dy * SIDE + dz
                first, second = kept(k, True)
                block = jnp.where(picks[source] == 0, pool[other, r, 0, :, cols], pool[other, r, 1, :, cols])
                top += across(first, block, ((1,), (0,)))
                low += across(second, block, ((1,), (0,)))
            out[0:blk, cols] = top
            out[blk:2 * blk, cols] = low

    def take_core(r):
        for b in range(2):
            to_core(r, b).wait_recv()

    def px_copy(d):
        rows = pl.ds(pl.multiple_of(((m + d) % SIDE) * x_rows, x_rows), x_rows)
        return remote(
            part_x_out.at[rows], part_x_in.at[d - 1], px_send.at[d - 1], px_recv.at[d - 1],
            {"member": (m + d) % SIDE},
        )

    def py_copy(d):
        rows = pl.ds(pl.multiple_of(((y + d) % SIDE) * y_rows, y_rows), y_rows)
        return remote(
            part_y.at[rows], part_y_in.at[d - 1], py_send.at[d - 1], py_recv.at[d - 1],
            {"group": at(d, 0)},
        )

    def pz_copy(d):
        return remote(
            part_z.at[z], part_z.at[z], pz_send.at[d - 1], pz_recv.at[d - 1], {"group": at(0, d)}
        )

    def ty_copy(d):
        rows = pl.ds(pl.multiple_of(y * y_rows, y_rows), y_rows)
        return remote(
            total_y.at[rows], total_y.at[rows], ty_send.at[d - 1], ty_recv.at[d - 1], {"group": at(d, 0)}
        )

    def tx_copy(d):
        rows = pl.ds(pl.multiple_of(c * half_rows + m * x_rows, x_rows), x_rows)
        return remote(
            total.at[rows], total.at[rows], tx_send.at[d - 1], tx_recv.at[d - 1],
            {"member": (m + d) % SIDE},
        )

    tc = remote(total.at[mine], total.at[mine], tc_send, tc_recv, partner)

    def launch(copies):
        for copy in copies:
            copy.start()
            sent.append(copy)

    def grad_step(number):
        peers = range(1, SIDE)
        if number == 0:
            pc.wait_recv()
            part[mine, :] += part_core[...]
            part_x_out[...] = part[mine, :].astype(jnp.bfloat16)
            launch([px_copy(d) for d in peers])
        elif number == 1:
            for d in peers:
                px_copy(d).wait_recv()
            rows = pl.ds(pl.multiple_of(c * half_rows + m * x_rows, x_rows), x_rows)
            summed = part[rows, :]
            for d in peers:
                summed += part_x_in[d - 1].astype(jnp.float32)
            part_y[...] = summed
            launch([py_copy(d) for d in peers])
        elif number == 2:
            for d in peers:
                py_copy(d).wait_recv()
            rows = pl.ds(pl.multiple_of(y * y_rows, y_rows), y_rows)
            summed = part_y[rows, :]
            for d in peers:
                summed += part_y_in[d - 1]
            part_z[z] = summed
            launch([pz_copy(d) for d in peers])
        elif number == 3:
            for d in peers:
                pz_copy(d).wait_recv()
            rows = pl.ds(pl.multiple_of(y * y_rows, y_rows), y_rows)
            total_y[rows, :] = (part_z[0] + part_z[1]) + (part_z[2] + part_z[3])
            launch([ty_copy(d) for d in peers])
        elif number == 4:
            for d in peers:
                ty_copy(d).wait_recv()
            rows = pl.ds(pl.multiple_of(c * half_rows + m * x_rows, x_rows), x_rows)
            total[rows, :] = total_y[...].astype(jnp.bfloat16)
            launch([tx_copy(d) for d in peers])
        elif number == 5:
            for d in peers:
                tx_copy(d).wait_recv()
            launch([tc])
        elif number == 6:
            tc.wait_recv()
            gout[...] = total[...].astype(jnp.float32)

    grad_step(0)
    take_core(0)
    sweep(1, ((0, 0),))
    grad_at = {1: 1, 2: 2, 3: 3, 4: 4, 6: 5, 7: 6}

    for number, (blocks, complete) in enumerate(ARRIVE):
        for dy, dz, b in blocks:
            for key in arrivals(dy, dz, b):
                ring(*key).wait_recv()
            forward(dy, dz, b)
        if number in grad_at:
            grad_step(grad_at[number])
        if number == 5:
            for d in range(1, SIDE):
                remote(
                    member_out.at[d - 1], member_in.at[2 + (m - d + SIDE) % SIDE], member_send.at[d - 1],
                    member_recv.at[d - 1], {"member": (m + d) % SIDE},
                ).wait_recv()

            @pl.loop(2 * SIDE * SIDE - 1, slot_total)
            def _(k):
                first, second = kept(k, k < count[0])

                @pl.loop(0, width // cut)
                def _(n):
                    cols = cols_of(n)
                    block = member_in[slots[k], :, cols]
                    out[0:blk, cols] += across(first, block, ((1,), (0,)))
                    out[blk:2 * blk, cols] += across(second, block, ((1,), (0,)))

        if complete:
            sweep(0, complete)
            for dy, dz in complete:
                take_core(dy * SIDE + dz)
            sweep(1, complete)

    for copy in sent:
        copy.wait_send()


def hop(picks, slots, targets, count, lists, agg, weight, grad, values, scale, interpret=False):
    rows, width = agg.shape
    slot_total, blk, _ = values.shape
    bf16, f32 = jnp.bfloat16, jnp.float32
    half_rows, x_rows = width // 2, width // 8
    y_rows = x_rows // SIDE
    vmem, smem = pl.BlockSpec(memory_space=pltpu.VMEM), pl.BlockSpec(memory_space=pltpu.SMEM)
    dma = pltpu.SemaphoreType.DMA
    return pl.pallas_call(
        functools.partial(hop_kernel, scale),
        out_shape=(jax.ShapeDtypeStruct((rows, width), f32), jax.ShapeDtypeStruct((width, width), f32)),
        in_specs=[smem] * 5 + [vmem] * 3 + [pl.BlockSpec(memory_space=pl.ANY)],
        out_specs=(vmem, vmem),
        scratch_shapes=[
            pltpu.VMEM((2, SIDE * SIDE, 2, blk, width), bf16),
            pltpu.VMEM((slot_total, blk, blk), bf16),
            pltpu.VMEM((SIDE - 1, blk, width), bf16),
            pltpu.VMEM((2 + SIDE, blk, width), bf16),
            pltpu.VMEM((rows, width), bf16),
            pltpu.VMEM((width, width), f32),
            pltpu.VMEM((half_rows, width), f32),
            pltpu.VMEM((half_rows, width), bf16),
            pltpu.VMEM((SIDE - 1, x_rows, width), bf16),
            pltpu.VMEM((x_rows, width), f32),
            pltpu.VMEM((SIDE - 1, y_rows, width), f32),
            pltpu.VMEM((SIDE, y_rows, width), f32),
            pltpu.VMEM((x_rows, width), f32),
            pltpu.VMEM((width, width), bf16),
            dma(()),
            dma((SIDE * SIDE, 2, 2)), dma((SIDE * SIDE, 2, 2)),
            dma((SIDE * SIDE, 2)), dma((SIDE * SIDE, 2)),
            dma((SIDE - 1,)), dma((SIDE - 1,)),
            dma(()), dma(()),
            dma((SIDE - 1,)), dma((SIDE - 1,)),
            dma((SIDE - 1,)), dma((SIDE - 1,)),
            dma((SIDE - 1,)), dma((SIDE - 1,)),
            dma((SIDE - 1,)), dma((SIDE - 1,)),
            dma((SIDE - 1,)), dma((SIDE - 1,)),
            dma(()), dma(()),
        ],
        compiler_params=pltpu.CompilerParams(
            collective_id=0, has_side_effects=True, vmem_limit_bytes=60 << 20
        ),
        name="hop",
    )(picks, slots, targets, count, lists, agg, weight, grad, values)


def body(
    agg_one,
    agg_two,
    grad_out,
    hop_one_weight,
    hop_two_weight,
    block_values,
    src_slot,
    dst_block,
    block_count,
    send_member,
    send_group,
):
    total_labels = agg_one.shape[0] * lax.axis_size("member") * lax.axis_size("group")
    scale = float(total_labels) ** (-0.5)
    picks = lax.all_to_all(send_group[0], "group", split_axis=0, concat_axis=0, tiled=True)
    graph = (picks, src_slot[0], dst_block[0], block_count, send_member[0, :, 0])
    carry, grad_w_two = hop(
        *graph, agg_two, hop_two_weight, grad_out.astype(jnp.float32), block_values, scale
    )
    emb, grad_w_one = hop(*graph, agg_one, hop_one_weight, carry, block_values, scale)
    return (emb.astype(jnp.bfloat16), grad_w_one, grad_w_two)


def solution(mesh):
    in_specs = (
        P(("member", "group"), None),
        P(("member", "group"), None),
        P(("member", "group"), None),
        P(),
        P(),
        P(("member", "group"), None, None),
        P(("member", "group"), None),
        P(("member", "group"), None),
        P(("member", "group")),
        P(("member", "group"), None, None),
        P(("member", "group"), None),
    )
    out_specs = (P(("member", "group"), None), P(), P())
    return jax.shard_map(body, mesh=mesh, in_specs=in_specs, out_specs=out_specs, check_vma=False)
```

```python
import functools

import jax
import jax.numpy as jnp
from jax import lax
from jax.experimental import pallas as pl
from jax.experimental.pallas import tpu as pltpu
from jax.sharding import PartitionSpec as P

MESH = pl.DeviceIdType.MESH
SIDE = 4

STEP_US = {"arrive": 0.12, "sweep": 0.7, "late": 0.7, "grad": 1.0}
LINK_US = 2 * 0.1966 / 0.090
X_US = LINK_US
CORE_US = 0.1966 / 0.3
DELAY_US = 1.5
LATE_PARTS = 8
QUEUE_US = 6.0


def onward(dy, dz, b, part):
    first, second = (0, 1) if b == 0 else (1, 0)
    pos = (dy, dz)

    def step(axis, way):
        new = list(pos)
        new[axis] = (new[axis] + way) % SIDE
        return (new[0], new[1], b, part, axis, way)

    d1, d2 = pos[first], pos[second]
    moved = []
    if d2 == 0:
        if d1 == 0:
            moved += [step(first, 1), step(first, -1)]
        elif (d1, part) == (1, 0):
            moved.append(step(first, 1))
        elif (d1, part) == (3, 1):
            moved.append(step(first, -1))
        moved += [step(second, 1), step(second, -1)]
    elif (d2, part) == (1, 0):
        moved.append(step(second, 1))
    elif (d2, part) == (3, 1):
        moved.append(step(second, -1))
    return moved


def own_copies():
    first, rest = {0: [], 1: []}, []
    for b in range(2):
        for part in range(2):
            moved = onward(0, 0, b, part)
            first[b] += moved[:2]
            rest += moved[2:]
    order = lambda key: (key[3] if key[5] == 1 else 1 - key[3])
    return sorted(first[0], key=order), sorted(first[1], key=order), sorted(rest, key=order)


def plan():
    free = {}
    here = {}

    def send(link, key, cost, now):
        start = max(free.get(link, 0.0), now)
        free[link] = start + cost
        here[key] = start + cost + DELAY_US

    held = []

    def flush():
        nonlocal now
        for key in sorted(held, key=lambda key: key[0] != 0 and key[1] != 0):
            if free.get(key[4:], 0.0) <= now + QUEUE_US:
                held.remove(key)
                result.append(("send",) + key)
                send(key[4:], ("ring",) + key[:4], LINK_US, now)
                waiting.add(key[:4])

    def send_core(key, now):
        send("core", ("core",) + key, CORE_US, now)

    def send_peers(axis, name, cost, now):
        send((axis, 1), (name, 1), cost, now)
        send((axis, -1), (name, 3), cost, now)
        send((axis, 1), (name, 2), 2 * cost, now)

    result, waiting = [], set()
    now = 6.0
    first, second, rest = own_copies()
    for key in first + second:
        send(key[4:], ("ring",) + key[:4], LINK_US, 1.5)
        waiting.add(key[:4])
    held += rest
    for b in range(2):
        for part in range(2):
            send_core((0, 0, b, part), 3.0)
    send("core", ("pc", 0), 6 * CORE_US, 5.0)
    flush()
    seen = {(0, 0, b, part) for b in range(2) for part in range(2)}
    tasks = [("grad", n) for n in range(7)]
    tasks += [("sweep", 0, dy, dz) for dy in range(SIDE) for dz in range(SIDE) if (dy, dz) != (0, 0)]
    tasks += [("sweep", 1, dy, dz) for dy in range(SIDE) for dz in range(SIDE)]
    tasks += [("late", n) for n in range(LATE_PARTS)]
    needs = {0: ["pc"], 1: ["px"], 2: ["py"], 3: ["pz"], 4: ["ty"], 5: ["tx"], 6: ["tc"]}
    done_grad = -1

    def ready(task):
        if task[0] == "grad":
            if task[1] != done_grad + 1:
                return 1e9
            names = needs[task[1]]
            times = [here[key] for key in here if key[0] in names]
            return max(times)
        if task[0] == "late":
            times = [here[key] for key in here if key[0] == "member"]
            return max(times) if times else 1e9
        _, other, dy, dz = task
        keys = [(dy, dz, b, part) for b in range(2) for part in range(2)]
        if other == 0:
            return 0.0 if all(key in seen for key in keys) else 1e9
        return max(here.get(("core",) + key, 1e9) for key in keys)

    def price(task):
        if task[0] == "late":
            return STEP_US["late"] * 17 / LATE_PARTS
        return STEP_US[task[0]]

    def run(task):
        nonlocal now, done_grad
        now = max(now, ready(task)) + price(task)
        result.append(task)
        tasks.remove(task)
        if task[0] == "grad":
            done_grad = n = task[1]
            if n == 0:
                send_peers("x", "px", X_US * 0.75, now)
                send_peers("x", "member", 2 * X_US, now)
            elif n == 1:
                send_peers(0, "py", 0.375 * LINK_US, now)
            elif n == 2:
                send_peers(1, "pz", 0.375 * LINK_US, now)
            elif n == 3:
                send_peers(0, "ty", 0.375 * LINK_US, now)
            elif n == 4:
                send_peers("x", "tx", X_US * 0.75, now)
            elif n == 5:
                send("core", ("tc", 0), 3 * CORE_US, now)

    while waiting or held:
        flush()
        coming = min(waiting, key=lambda key: (here[("ring",) + key], key))
        arrival = here[("ring",) + coming]
        if arrival > now:
            able = [task for task in tasks if ready(task) <= now]
            able = [task for task in able if now + price(task) <= arrival + 0.5]
            if able:
                run(able[0])
                flush()
                continue
            soon = [task for task in tasks if task[0] == "grad" and ready(task) + 0.2 <= arrival]
            if soon:
                run(soon[0])
                flush()
                continue
        now = max(now, arrival) + STEP_US["arrive"]
        waiting.remove(coming)
        seen.add(coming)
        result.append(("arrive",) + coming)
        held += onward(*coming)
        flush()
        send_core(coming, now)
    while tasks:
        run(min(tasks, key=lambda task: (ready(task), task[0])))
    return result, now


def slope(value):
    sig = jax.nn.sigmoid(value)
    return sig * (1.0 + value * (1.0 - sig))


def across(left, right, dims):
    return lax.dot_general(left, right, (dims, ((), ())), preferred_element_type=jnp.float32)


def hop_kernel(scale, is_first, *refs):
    (slots, targets, count, lists, picks_in, agg, weight, grad, values_hbm), refs = refs[:9], refs[9:]
    out_ref, gout = refs[:2]
    refs = refs[2:]
    if is_first:
        picks_out, refs = refs[0], refs[1:]
    (
        pool, values, lhs, member_out, member_in, pull,
        part, part_core, part_x_out, part_x_in, part_y, part_y_in, part_z, total_y, total,
        values_sem, ring_send, ring_recv, core_send, core_recv, member_send, member_recv,
        pc_send, pc_recv, px_send, px_recv, py_send, py_recv, pz_send, pz_recv,
        ty_send, ty_recv, tx_send, tx_recv, tc_send, tc_recv,
    ), refs = refs[:36], refs[36:]
    if is_first:
        out = out_ref
        table, table_smem, picks_sem, kc_send, kc_recv, ky_send, ky_recv, kz_send, kz_recv = refs
        picks = picks_out
    else:
        (out,) = refs
        picks = picks_in
    blk = values.shape[1]
    width = weight.shape[0]
    slot_total = values.shape[0]
    half = blk // 2
    cut = min(256, width)
    m = lax.axis_index("member")
    g = lax.axis_index("group")
    y, z, c = g // (2 * SIDE), (g // 2) % SIDE, g % 2
    peers = range(1, SIDE)

    def at(dy, dz, other=0):
        core = c if other == 0 else 1 - c
        return (((y + dy) % SIDE) * SIDE + (z + dz) % SIDE) * 2 + core

    partner = {"group": at(0, 0, 1)}

    load_values = pltpu.make_async_copy(values_hbm, values, values_sem)
    load_values.start()

    barrier = pltpu.get_barrier_semaphore()
    for d in peers:
        for peer in ({"group": at(d, 0)}, {"group": at(0, d)}, {"member": (m + d) % SIDE}):
            pl.semaphore_signal(barrier, inc=1, device_id=peer, device_id_type=MESH)
    pl.semaphore_signal(barrier, inc=1, device_id=partner, device_id_type=MESH)

    def remote(src, dst, send, recv, peer):
        return pltpu.make_async_remote_copy(
            src_ref=src, dst_ref=dst, send_sem=send, recv_sem=recv, device_id=peer, device_id_type=MESH
        )

    sent = []

    def launch(copies):
        for copy in copies:
            copy.start()
            sent.append(copy)

    def ring(dy, dz, b, half_no, axis, way):
        rows = pl.ds(half_no * half, half)
        sdy, sdz = ((dy - way) % SIDE, dz) if axis == 0 else (dy, (dz - way) % SIDE)
        return remote(
            pool.at[0, sdy * SIDE + sdz, b, rows],
            pool.at[0, dy * SIDE + dz, b, rows],
            ring_send.at[dy * SIDE + dz, b, half_no],
            ring_recv.at[dy * SIDE + dz, b, half_no],
            {"group": at(way, 0) if axis == 0 else at(0, way)},
        )

    def wait_half(dy, dz, b, half_no):
        axis, d = (1, dz) if b == 0 else (0, dy)
        if d == 0:
            axis, d = (0, dy) if b == 0 else (1, dz)
        way = {1: 1, 3: -1, 2: 1 - 2 * half_no}[d]
        ring(dy, dz, b, half_no, axis, way).wait_recv()

    def to_core(dy, dz, b, half_no):
        rows = pl.ds(half_no * half, half)
        r = dy * SIDE + dz
        return remote(
            pool.at[0, r, b, rows], pool.at[1, r, b, rows],
            core_send.at[r, b, half_no], core_recv.at[r, b, half_no], partner,
        )

    if is_first:
        kc = remote(table.at[0, 0, 0], table.at[0, 0, 1], kc_send, kc_recv, partner)
        ky = [
            remote(table.at[0, 0], table.at[0, d], ky_send.at[d - 1], ky_recv.at[d - 1], {"group": at(d, 0)})
            for d in peers
        ]
        kz = [
            remote(table.at[0], table.at[d], kz_send.at[d - 1], kz_recv.at[d - 1], {"group": at(0, d)})
            for d in peers
        ]
        table[0, 0, 0] = jnp.broadcast_to(picks_in[...], table.shape[3:])

    rows_at = min(128, blk)
    own_first = own_copies()

    def own_block(b):
        @pl.loop(0, blk // rows_at)
        def _(i):
            inner = pl.ds(pl.multiple_of(i * rows_at, rows_at), rows_at)
            rows = pl.ds(pl.multiple_of(b * blk + i * rows_at, rows_at), rows_at)
            lift = across(agg[rows, :], weight[...], ((1,), (0,)))
            pulled = (grad[rows, :].astype(jnp.float32) * slope(lift)).astype(jnp.bfloat16)
            pull[rows, :] = pulled
            back = across(pulled, weight[...], ((1,), (1,))).astype(jnp.bfloat16)
            pool[0, 0, b, inner, :] = back

    pl.semaphore_wait(barrier, 3 * (SIDE - 1) + 1)
    if is_first:
        launch([kc])
    own_block(0)
    if is_first:
        kc.wait_recv()
        launch(ky)
    launch([ring(*key) for key in own_first[0]])
    own_block(1)
    if is_first:
        for copy in ky:
            copy.wait_recv()
        launch(kz)
    launch([ring(*key) for key in own_first[1]])
    order = plan()[0]
    while order[0][0] == "send":
        launch([ring(*order.pop(0)[1:])])
    launch([to_core(0, 0, b, part_no) for b in range(2) for part_no in range(2)])

    half_rows, x_rows = width // 2, width // 8
    y_rows = x_rows // SIDE

    @pl.loop(0, width // cut)
    def _(i):
        rows = pl.ds(pl.multiple_of(i * cut, cut), cut)
        part[rows, :] = across(agg[:, rows], pull[...], ((0,), (0,))) * scale

    mine = pl.ds(pl.multiple_of(c * half_rows, half_rows), half_rows)
    theirs = pl.ds(pl.multiple_of((1 - c) * half_rows, half_rows), half_rows)
    pc = remote(part.at[theirs], part_core, pc_send, pc_recv, partner)
    launch([pc])

    for d in peers:
        member_out[d - 1] = jnp.where(lists[(m + d) % SIDE] == 0, pool[0, 0, 0], pool[0, 0, 1])
    member_in[0] = pool[0, 0, 0]
    member_in[1] = pool[0, 0, 1]
    member_in[2 + m] = jnp.where(lists[m] == 0, pool[0, 0, 0], pool[0, 0, 1])
    out[...] = grad[...].astype(jnp.float32)
    load_values.wait()

    def member_copy(d, source):
        return remote(
            member_out.at[d - 1], member_in.at[2 + source], member_send.at[d - 1], member_recv.at[d - 1],
            {"member": (m + d) % SIDE},
        )

    def set_lhs(k, live):
        value = values[k].T
        zero = jnp.zeros_like(value)
        where = targets[k]
        lhs[0:blk, :] = jnp.where(jnp.logical_and(live, where == 0), value, zero)
        lhs[blk:2 * blk, :] = jnp.where(jnp.logical_and(live, where == 1), value, zero)

    def take_picks():
        for copy in kz:
            copy.wait_recv()
        fetch = pltpu.make_async_copy(table, table_smem, picks_sem)
        fetch.start()
        fetch.wait()
        for other in range(2):
            for dy in range(SIDE):
                for dz in range(SIDE):
                    picks_out[other * SIDE * SIDE + dy * SIDE + dz] = table_smem[dz, dy, other, 0, g]

    picks_here = [not is_first]

    def sweep(other, dy, dz):
        if not picks_here[0]:
            take_picks()
            picks_here[0] = True
        if other == 1:
            for b in range(2):
                for part_no in range(2):
                    to_core(dy, dz, b, part_no).wait_recv()
        groups = 2 * SIDE * SIDE
        r = dy * SIDE + dz
        set_lhs((at(-dy, -dz, other) - g - 1 + groups) % groups, True)
        pick = picks[other * SIDE * SIDE + r]

        for n in range(width // cut):
            cols = pl.ds(n * cut, cut)
            block = jnp.where(pick == 0, pool[other, r, 0, :, cols], pool[other, r, 1, :, cols])
            out[:, cols] += across(lhs[...], block, ((1,), (0,)))

    def late(number):
        start = 2 * SIDE * SIDE - 1
        total_late = slot_total - start
        if number == 0:
            for d in peers:
                member_copy(d, (m - d + SIDE) % SIDE).wait_recv()

        @pl.loop(start + total_late * number // LATE_PARTS, start + total_late * (number + 1) // LATE_PARTS)
        def _(k):
            set_lhs(k, k < count[0])

            for n in range(width // cut):
                cols = pl.ds(n * cut, cut)
                out[:, cols] += across(lhs[...], member_in[slots[k], :, cols], ((1,), (0,)))

    def px_copy(d):
        rows = pl.ds(pl.multiple_of(((m + d) % SIDE) * x_rows, x_rows), x_rows)
        return remote(
            part_x_out.at[rows], part_x_in.at[d - 1], px_send.at[d - 1], px_recv.at[d - 1],
            {"member": (m + d) % SIDE},
        )

    def py_copy(d):
        rows = pl.ds(pl.multiple_of(((y + d) % SIDE) * y_rows, y_rows), y_rows)
        return remote(
            part_y.at[rows], part_y_in.at[d - 1], py_send.at[d - 1], py_recv.at[d - 1],
            {"group": at(d, 0)},
        )

    def pz_copy(d, place):
        return remote(
            part_z.at[z], part_z.at[place], pz_send.at[d - 1], pz_recv.at[d - 1], {"group": at(0, d)}
        )

    def ty_copy(d, place):
        rows = pl.ds(pl.multiple_of(y * y_rows, y_rows), y_rows)
        there = pl.ds(pl.multiple_of(place * y_rows, y_rows), y_rows)
        return remote(
            total_y.at[rows], total_y.at[there], ty_send.at[d - 1], ty_recv.at[d - 1], {"group": at(d, 0)}
        )

    def tx_copy(d, place):
        rows = pl.ds(pl.multiple_of(c * half_rows + m * x_rows, x_rows), x_rows)
        there = pl.ds(pl.multiple_of(c * half_rows + place * x_rows, x_rows), x_rows)
        return remote(
            total.at[rows], total.at[there], tx_send.at[d - 1], tx_recv.at[d - 1],
            {"member": (m + d) % SIDE},
        )

    def tc_copy(there):
        return remote(total.at[mine], total.at[there], tc_send, tc_recv, partner)

    x_mine = pl.ds(pl.multiple_of(c * half_rows + m * x_rows, x_rows), x_rows)
    y_mine = pl.ds(pl.multiple_of(y * y_rows, y_rows), y_rows)

    def grad_step(number):
        if number == 0:
            pc.wait_recv()
            part[mine, :] += part_core[...]
            part_x_out[...] = part[mine, :].astype(jnp.bfloat16)
            launch([px_copy(d) for d in peers])
            launch([member_copy(d, m) for d in peers])
        elif number == 1:
            for d in peers:
                px_copy(d).wait_recv()
            summed = part[x_mine, :]
            for d in peers:
                summed += part_x_in[d - 1].astype(jnp.float32)
            part_y[...] = summed
            launch([py_copy(d) for d in peers])
        elif number == 2:
            for d in peers:
                py_copy(d).wait_recv()
            summed = part_y[y_mine, :]
            for d in peers:
                summed += part_y_in[d - 1]
            part_z[z] = summed
            launch([pz_copy(d, z) for d in peers])
        elif number == 3:
            for d in peers:
                pz_copy(d, (z - d + SIDE) % SIDE).wait_recv()
            total_y[y_mine, :] = (part_z[0] + part_z[1]) + (part_z[2] + part_z[3])
            launch([ty_copy(d, y) for d in peers])
        elif number == 4:
            for d in peers:
                ty_copy(d, (y - d + SIDE) % SIDE).wait_recv()
            total[x_mine, :] = total_y[...].astype(jnp.bfloat16)
            launch([tx_copy(d, m) for d in peers])
        elif number == 5:
            for d in peers:
                tx_copy(d, (m - d + SIDE) % SIDE).wait_recv()
            launch([tc_copy(mine)])
        elif number == 6:
            tc_copy(theirs).wait_recv()
            gout[...] = total[...].astype(jnp.float32)

    for task in order:
        if task[0] == "arrive":
            wait_half(*task[1:])
            launch([to_core(*task[1:])])
        elif task[0] == "send":
            launch([ring(*task[1:])])
        elif task[0] == "sweep":
            sweep(*task[1:])
        elif task[0] == "late":
            late(task[1])
        else:
            grad_step(task[1])

    if not is_first:
        out_ref[...] = out[...].astype(out_ref.dtype)
    for copy in sent:
        copy.wait_send()


def hop(is_first, slots, targets, count, lists, picks, agg, weight, grad, values, scale):
    rows, width = agg.shape
    slot_total, blk, _ = values.shape
    bf16, f32, i32 = jnp.bfloat16, jnp.float32, jnp.int32
    half_rows, x_rows = width // 2, width // 8
    y_rows = x_rows // SIDE
    vmem, smem = pl.BlockSpec(memory_space=pltpu.VMEM), pl.BlockSpec(memory_space=pltpu.SMEM)
    dma = pltpu.SemaphoreType.DMA
    peers = dma((SIDE - 1,))
    out_shape = [
        jax.ShapeDtypeStruct((rows, width), f32 if is_first else bf16),
        jax.ShapeDtypeStruct((width, width), f32),
    ]
    out_specs = [vmem, vmem]
    scratch = [
        pltpu.VMEM((2, SIDE * SIDE, 2, blk, width), bf16),
        pltpu.VMEM((slot_total, blk, blk), bf16),
        pltpu.VMEM((2 * blk, blk), bf16),
        pltpu.VMEM((SIDE - 1, blk, width), bf16),
        pltpu.VMEM((2 + SIDE, blk, width), bf16),
        pltpu.VMEM((rows, width), bf16),
        pltpu.VMEM((width, width), f32),
        pltpu.VMEM((half_rows, width), f32),
        pltpu.VMEM((half_rows, width), bf16),
        pltpu.VMEM((SIDE - 1, x_rows, width), bf16),
        pltpu.VMEM((x_rows, width), f32),
        pltpu.VMEM((SIDE - 1, y_rows, width), f32),
        pltpu.VMEM((SIDE, y_rows, width), f32),
        pltpu.VMEM((x_rows, width), f32),
        pltpu.VMEM((width, width), bf16),
        dma(()),
        dma((SIDE * SIDE, 2, 2)), dma((SIDE * SIDE, 2, 2)),
        dma((SIDE * SIDE, 2, 2)), dma((SIDE * SIDE, 2, 2)),
        peers, peers, dma(()), dma(()),
        peers, peers, peers, peers, peers, peers, peers, peers, peers, peers, dma(()), dma(()),
    ]
    if is_first:
        out_shape.append(jax.ShapeDtypeStruct((2 * SIDE * SIDE,), i32))
        out_specs.append(smem)
        scratch += [
            pltpu.VMEM((SIDE, SIDE, 2, 8, 128), i32),
            pltpu.SMEM((SIDE, SIDE, 2, 8, 128), i32),
            dma(()), dma(()), dma(()), peers, peers, peers, peers,
        ]
    else:
        scratch.append(pltpu.VMEM((rows, width), f32))
    return pl.pallas_call(
        functools.partial(hop_kernel, scale, is_first),
        out_shape=tuple(out_shape),
        in_specs=[smem] * 4 + [vmem if is_first else smem] + [vmem] * 3 + [pl.BlockSpec(memory_space=pl.ANY)],
        out_specs=tuple(out_specs),
        scratch_shapes=scratch,
        compiler_params=pltpu.CompilerParams(
            collective_id=0 if is_first else 1, has_side_effects=True, vmem_limit_bytes=60 << 20
        ),
        name="hop_two" if is_first else "hop_one",
    )(slots, targets, count, lists, picks, agg, weight, grad, values)


def body(
    agg_one,
    agg_two,
    grad_out,
    hop_one_weight,
    hop_two_weight,
    block_values,
    src_slot,
    dst_block,
    block_count,
    send_member,
    send_group,
):
    total_labels = agg_one.shape[0] * lax.axis_size("member") * lax.axis_size("group")
    scale = float(total_labels) ** (-0.5)
    graph = (src_slot[0], dst_block[0], block_count, send_member[0, :, 0])
    listed = jnp.pad(send_group, ((0, 0), (0, 128 - send_group.shape[1])))
    carry, grad_w_two, picks = hop(
        True, *graph, listed, agg_two, hop_two_weight, grad_out, block_values, scale
    )
    emb, grad_w_one = hop(
        False, *graph, picks, agg_one, hop_one_weight, carry, block_values, scale
    )
    return (emb, grad_w_one, grad_w_two)


def solution(mesh):
    in_specs = (
        P(("member", "group"), None),
        P(("member", "group"), None),
        P(("member", "group"), None),
        P(),
        P(),
        P(("member", "group"), None, None),
        P(("member", "group"), None),
        P(("member", "group"), None),
        P(("member", "group")),
        P(("member", "group"), None, None),
        P(("member", "group"), None),
    )
    out_specs = (P(("member", "group"), None), P(), P())
    return jax.shard_map(body, mesh=mesh, in_specs=in_specs, out_specs=out_specs, check_vma=False)
```

```python
import functools

import jax
import jax.numpy as jnp
from jax import lax
from jax.experimental import pallas as pl
from jax.experimental.pallas import tpu as pltpu
from jax.sharding import PartitionSpec as P

MESH = pl.DeviceIdType.MESH
SIDE = 4

STEP_US = {"arrive": 0.12, "sweep": 0.7, "late": 0.7, "grad": 1.0}
LINK_US = 2 * 0.1966 / 0.090
X_US = LINK_US
CORE_US = 0.1966 / 0.3
DELAY_US = 1.5
LATE_PARTS = 8
QUEUE_US = 4.0


def onward(dy, dz, b, part):
    first, second = (0, 1) if b == 0 else (1, 0)
    pos = (dy, dz)

    def step(axis, way):
        new = list(pos)
        new[axis] = (new[axis] + way) % SIDE
        return (new[0], new[1], b, part, axis, way)

    d1, d2 = pos[first], pos[second]
    moved = []
    if d2 == 0:
        if d1 == 0:
            moved += [step(first, 1), step(first, -1)]
        elif (d1, part) == (1, 0):
            moved.append(step(first, 1))
        elif (d1, part) == (3, 1):
            moved.append(step(first, -1))
        moved += [step(second, 1), step(second, -1)]
    elif (d2, part) == (1, 0):
        moved.append(step(second, 1))
    elif (d2, part) == (3, 1):
        moved.append(step(second, -1))
    return moved


def own_copies():
    early = [
        [(1, 0, 0, 0, 0, 1), (0, 1, 0, 0, 1, 1)],
        [(3, 0, 0, 1, 0, -1), (0, 3, 0, 1, 1, -1), (1, 0, 0, 1, 0, 1), (3, 0, 0, 0, 0, -1)],
        [(0, 1, 1, 0, 1, 1)],
        [(0, 3, 1, 1, 1, -1), (0, 1, 1, 1, 1, 1), (0, 3, 1, 0, 1, -1)],
    ]
    rest = [key for b in range(2) for part in range(2) for key in onward(0, 0, b, part)]
    for group in early:
        for key in group:
            rest.remove(key)
    return early, sorted(rest, key=lambda key: key[3] if key[5] == 1 else 1 - key[3])


def plan():
    free = {}
    here = {}

    def send(link, key, cost, now):
        start = max(free.get(link, 0.0), now)
        free[link] = start + cost
        here[key] = start + cost + DELAY_US

    held = []

    def flush():
        nonlocal now
        for key in sorted(held, key=lambda key: key[0] != 0 and key[1] != 0):
            if free.get(key[4:], 0.0) <= now + QUEUE_US:
                held.remove(key)
                result.append(("send",) + key)
                send(key[4:], ("ring",) + key[:4], LINK_US, now)
                waiting.add(key[:4])

    def send_core(key, now):
        send("core", ("core",) + key, CORE_US, now)

    def send_peers(axis, name, cost, now):
        send((axis, 1), (name, 1), cost, now)
        send((axis, -1), (name, 3), cost, now)
        send((axis, 1), (name, 2), 2 * cost, now)

    result, waiting = [], set()
    now = 6.0
    early, rest = own_copies()
    for number, group in enumerate(early):
        for key in group:
            send(key[4:], ("ring",) + key[:4], LINK_US, 1.5 + number)
            waiting.add(key[:4])
    held += rest
    for b in range(2):
        for part in range(2):
            send_core((0, 0, b, part), 3.0)
    send("core", ("pc", 0), 6 * CORE_US, 5.0)
    flush()
    seen = {(0, 0, b, part) for b in range(2) for part in range(2)}
    tasks = [("grad", n) for n in range(7)]
    tasks += [("sweep", 0, dy, dz) for dy in range(SIDE) for dz in range(SIDE) if (dy, dz) != (0, 0)]
    tasks += [("sweep", 1, dy, dz) for dy in range(SIDE) for dz in range(SIDE)]
    tasks += [("late", n) for n in range(LATE_PARTS)]
    needs = {0: ["pc"], 1: ["px"], 2: ["py"], 3: ["pz"], 4: ["ty"], 5: ["tx"], 6: ["tc"]}
    done_grad = -1

    def ready(task):
        if task[0] == "grad":
            if task[1] != done_grad + 1:
                return 1e9
            names = needs[task[1]]
            times = [here[key] for key in here if key[0] in names]
            return max(times)
        if task[0] == "late":
            times = [here[key] for key in here if key[0] == "member"]
            return max(times) if times else 1e9
        _, other, dy, dz = task
        keys = [(dy, dz, b, part) for b in range(2) for part in range(2)]
        if other == 0:
            return 0.0 if all(key in seen for key in keys) else 1e9
        return max(here.get(("core",) + key, 1e9) for key in keys)

    def price(task):
        if task[0] == "late":
            return STEP_US["late"] * 17 / LATE_PARTS
        return STEP_US[task[0]]

    def run(task):
        nonlocal now, done_grad
        now = max(now, ready(task)) + price(task)
        result.append(task)
        tasks.remove(task)
        if task[0] == "grad":
            done_grad = n = task[1]
            if n == 0:
                send_peers("x", "px", X_US * 0.75, now)
                send_peers("x", "member", 2 * X_US, now)
            elif n == 1:
                send_peers(0, "py", 0.1875 * LINK_US, now)
            elif n == 2:
                send_peers(1, "pz", 0.1875 * LINK_US, now)
            elif n == 3:
                send_peers(0, "ty", 0.1875 * LINK_US, now)
            elif n == 4:
                send_peers("x", "tx", X_US * 0.75, now)
            elif n == 5:
                send("core", ("tc", 0), 3 * CORE_US, now)

    while waiting or held:
        flush()
        coming = min(waiting, key=lambda key: (here[("ring",) + key], key))
        arrival = here[("ring",) + coming]
        if arrival > now:
            able = [task for task in tasks if ready(task) <= now]
            able = [task for task in able if now + price(task) <= arrival + 0.5]
            if able:
                run(able[0])
                flush()
                continue
            soon = [task for task in tasks if task[0] == "grad" and ready(task) + 0.2 <= arrival]
            if soon:
                run(soon[0])
                flush()
                continue
        now = max(now, arrival) + STEP_US["arrive"]
        waiting.remove(coming)
        seen.add(coming)
        result.append(("arrive",) + coming)
        held += onward(*coming)
        flush()
        send_core(coming, now)
    while tasks:
        run(min(tasks, key=lambda task: (ready(task), task[0])))
    return result, now


def slope(value):
    sig = jax.nn.sigmoid(value)
    return sig * (1.0 + value * (1.0 - sig))


def across(left, right, dims):
    return lax.dot_general(left, right, (dims, ((), ())), preferred_element_type=jnp.float32)


def hop_kernel(scale, is_first, *refs):
    (slots, targets, count, lists, picks_in, agg, weight, grad, values_hbm), refs = refs[:9], refs[9:]
    out_ref, total = refs[:2]
    refs = refs[2:]
    if is_first:
        picks_out, refs = refs[0], refs[1:]
    (
        pool, values, lhs, member_out, member_in, pull,
        part, part_core, part_x_out, part_x_in, part_y, part_y_in, part_z, total_y,
        values_sem, ring_send, ring_recv, core_send, core_recv, member_send, member_recv,
        pc_send, pc_recv, px_send, px_recv, py_send, py_recv, pz_send, pz_recv,
        ty_send, ty_recv, tx_send, tx_recv, tc_send, tc_recv,
    ), refs = refs[:35], refs[35:]
    if is_first:
        out = out_ref
        table, table_smem, picks_sem, kc_send, kc_recv, ky_send, ky_recv, kz_send, kz_recv = refs
        picks = picks_out
    else:
        (out,) = refs
        picks = picks_in
    blk = values.shape[1]
    width = weight.shape[0]
    slot_total = values.shape[0]
    half = blk // 2
    cut = min(256, width)
    m = lax.axis_index("member")
    g = lax.axis_index("group")
    y, z, c = g // (2 * SIDE), (g // 2) % SIDE, g % 2
    peers = range(1, SIDE)

    def at(dy, dz, other=0):
        core = c if other == 0 else 1 - c
        return (((y + dy) % SIDE) * SIDE + (z + dz) % SIDE) * 2 + core

    partner = {"group": at(0, 0, 1)}

    load_values = pltpu.make_async_copy(values_hbm, values, values_sem)
    load_values.start()

    barrier = pltpu.get_barrier_semaphore()
    for d in peers:
        for peer in ({"group": at(d, 0)}, {"group": at(0, d)}, {"member": (m + d) % SIDE}):
            pl.semaphore_signal(barrier, inc=1, device_id=peer, device_id_type=MESH)
    pl.semaphore_signal(barrier, inc=1, device_id=partner, device_id_type=MESH)

    def remote(src, dst, send, recv, peer):
        return pltpu.make_async_remote_copy(
            src_ref=src, dst_ref=dst, send_sem=send, recv_sem=recv, device_id=peer, device_id_type=MESH
        )

    sent = []

    def launch(copies):
        for copy in copies:
            copy.start()
            sent.append(copy)

    def ring(dy, dz, b, half_no, axis, way):
        rows = pl.ds(half_no * half, half)
        sdy, sdz = ((dy - way) % SIDE, dz) if axis == 0 else (dy, (dz - way) % SIDE)
        return remote(
            pool.at[0, sdy * SIDE + sdz, b, rows],
            pool.at[0, dy * SIDE + dz, b, rows],
            ring_send.at[dy * SIDE + dz, b, half_no],
            ring_recv.at[dy * SIDE + dz, b, half_no],
            {"group": at(way, 0) if axis == 0 else at(0, way)},
        )

    def wait_half(dy, dz, b, half_no):
        axis, d = (1, dz) if b == 0 else (0, dy)
        if d == 0:
            axis, d = (0, dy) if b == 0 else (1, dz)
        way = {1: 1, 3: -1, 2: 1 - 2 * half_no}[d]
        ring(dy, dz, b, half_no, axis, way).wait_recv()

    def to_core(dy, dz, b, half_no):
        rows = pl.ds(half_no * half, half)
        r = dy * SIDE + dz
        return remote(
            pool.at[0, r, b, rows], pool.at[1, r, b, rows],
            core_send.at[r, b, half_no], core_recv.at[r, b, half_no], partner,
        )

    if is_first:
        kc = remote(table.at[0, 0, 0], table.at[0, 0, 1], kc_send, kc_recv, partner)
        ky = [
            remote(table.at[0, 0], table.at[0, d], ky_send.at[d - 1], ky_recv.at[d - 1], {"group": at(d, 0)})
            for d in peers
        ]
        kz = [
            remote(table.at[0], table.at[d], kz_send.at[d - 1], kz_recv.at[d - 1], {"group": at(0, d)})
            for d in peers
        ]
        table[0, 0, 0] = jnp.zeros(table.shape[3:], jnp.int32)
        table[0, 0, 0, 0:1, 0:picks_in.shape[1]] = picks_in[...]

    early = own_copies()[0]

    def own_part(b, part_no):
        rows = pl.ds(b * blk + part_no * half, half)
        lift = across(agg[rows, :], weight[...], ((1,), (0,)))
        pulled = (grad[rows, :].astype(jnp.float32) * slope(lift)).astype(jnp.bfloat16)
        pull[rows, :] = pulled
        back = across(pulled, weight[...], ((1,), (1,))).astype(jnp.bfloat16)
        pool[0, 0, b, pl.ds(part_no * half, half), :] = back
        launch([ring(*key) for key in early[b * 2 + part_no]])

    pl.semaphore_wait(barrier, 3 * (SIDE - 1) + 1)
    if is_first:
        launch([kc])
    own_part(0, 0)
    if is_first:
        kc.wait_recv()
        launch(ky)
    own_part(0, 1)
    own_part(1, 0)
    if is_first:
        for copy in ky:
            copy.wait_recv()
        launch(kz)
    own_part(1, 1)
    order = plan()[0]
    while order[0][0] == "send":
        launch([ring(*order.pop(0)[1:])])
    launch([to_core(0, 0, b, part_no) for b in range(2) for part_no in range(2)])

    half_rows, x_rows = width // 2, width // 8
    lanes = width // 128
    y_rows = x_rows * lanes // SIDE

    @pl.loop(0, width // cut)
    def _(i):
        rows = pl.ds(pl.multiple_of(i * cut, cut), cut)
        part[rows, :] = across(agg[:, rows], pull[...], ((0,), (0,))) * scale

    mine = pl.ds(pl.multiple_of(c * half_rows, half_rows), half_rows)
    theirs = pl.ds(pl.multiple_of((1 - c) * half_rows, half_rows), half_rows)
    pc = remote(part.at[theirs], part_core, pc_send, pc_recv, partner)
    launch([pc])

    for d in peers:
        member_out[d - 1] = jnp.where(lists[(m + d) % SIDE] == 0, pool[0, 0, 0], pool[0, 0, 1])
    member_in[0] = pool[0, 0, 0]
    member_in[1] = pool[0, 0, 1]
    member_in[2 + m] = jnp.where(lists[m] == 0, pool[0, 0, 0], pool[0, 0, 1])
    out[...] = grad[...].astype(jnp.float32)
    load_values.wait()

    def member_copy(d, source):
        return remote(
            member_out.at[d - 1], member_in.at[2 + source], member_send.at[d - 1], member_recv.at[d - 1],
            {"member": (m + d) % SIDE},
        )

    def set_lhs(k, live):
        value = values[k].T
        zero = jnp.zeros_like(value)
        where = targets[k]
        lhs[0:blk, :] = jnp.where(jnp.logical_and(live, where == 0), value, zero)
        lhs[blk:2 * blk, :] = jnp.where(jnp.logical_and(live, where == 1), value, zero)

    def take_picks():
        for copy in kz:
            copy.wait_recv()
        fetch = pltpu.make_async_copy(table.at[:, :, :, pl.ds(0, 1)], table_smem, picks_sem)
        fetch.start()
        fetch.wait()
        for other in range(2):
            for dy in range(SIDE):
                for dz in range(SIDE):
                    picks_out[other * SIDE * SIDE + dy * SIDE + dz] = table_smem[dz, dy, other, 0, g]

    picks_here = [not is_first]

    def sweep(other, dy, dz):
        if not picks_here[0]:
            take_picks()
            picks_here[0] = True
        if other == 1:
            for b in range(2):
                for part_no in range(2):
                    to_core(dy, dz, b, part_no).wait_recv()
        groups = 2 * SIDE * SIDE
        r = dy * SIDE + dz
        set_lhs((at(-dy, -dz, other) - g - 1 + groups) % groups, True)
        pick = picks[other * SIDE * SIDE + r]

        for n in range(width // cut):
            cols = pl.ds(n * cut, cut)
            block = jnp.where(pick == 0, pool[other, r, 0, :, cols], pool[other, r, 1, :, cols])
            out[:, cols] += across(lhs[...], block, ((1,), (0,)))

    def late(number):
        start = 2 * SIDE * SIDE - 1
        total_late = slot_total - start
        if number == 0:
            for d in peers:
                member_copy(d, (m - d + SIDE) % SIDE).wait_recv()

        @pl.loop(start + total_late * number // LATE_PARTS, start + total_late * (number + 1) // LATE_PARTS)
        def _(k):
            set_lhs(k, k < count[0])

            for n in range(width // cut):
                cols = pl.ds(n * cut, cut)
                out[:, cols] += across(lhs[...], member_in[slots[k], :, cols], ((1,), (0,)))

    def px_copy(d):
        rows = pl.ds(pl.multiple_of(((m + d) % SIDE) * x_rows, x_rows), x_rows)
        return remote(
            part_x_out.at[rows], part_x_in.at[d - 1], px_send.at[d - 1], px_recv.at[d - 1],
            {"member": (m + d) % SIDE},
        )

    def py_copy(d):
        rows = pl.ds(pl.multiple_of(((y + d) % SIDE) * y_rows, y_rows), y_rows)
        return remote(
            part_y.at[rows], part_y_in.at[d - 1], py_send.at[d - 1], py_recv.at[d - 1],
            {"group": at(d, 0)},
        )

    def pz_copy(d, place):
        return remote(
            part_z.at[z], part_z.at[place], pz_send.at[d - 1], pz_recv.at[d - 1], {"group": at(0, d)}
        )

    def ty_copy(d, place):
        rows = pl.ds(pl.multiple_of(y * y_rows, y_rows), y_rows)
        there = pl.ds(pl.multiple_of(place * y_rows, y_rows), y_rows)
        return remote(
            total_y.at[rows], total_y.at[there], ty_send.at[d - 1], ty_recv.at[d - 1], {"group": at(d, 0)}
        )

    def tx_copy(d, place):
        rows = pl.ds(pl.multiple_of(c * half_rows + m * x_rows, x_rows), x_rows)
        there = pl.ds(pl.multiple_of(c * half_rows + place * x_rows, x_rows), x_rows)
        return remote(
            total.at[rows], total.at[there], tx_send.at[d - 1], tx_recv.at[d - 1],
            {"member": (m + d) % SIDE},
        )

    def tc_copy(there):
        return remote(total.at[mine], total.at[there], tc_send, tc_recv, partner)

    x_mine = pl.ds(pl.multiple_of(c * half_rows + m * x_rows, x_rows), x_rows)
    y_mine = pl.ds(pl.multiple_of(y * y_rows, y_rows), y_rows)

    def grad_step(number):
        if number == 0:
            pc.wait_recv()
            part[mine, :] += part_core[...]
            part_x_out[...] = part[mine, :].astype(jnp.bfloat16)
            launch([px_copy(d) for d in peers])
            launch([member_copy(d, m) for d in peers])
        elif number == 1:
            for d in peers:
                px_copy(d).wait_recv()
            summed = part[x_mine, :]
            for d in peers:
                summed += part_x_in[d - 1].astype(jnp.float32)
            for j in range(lanes):
                part_y[j * x_rows:(j + 1) * x_rows, :] = summed[:, j * 128:(j + 1) * 128].astype(jnp.bfloat16)
            launch([py_copy(d) for d in peers])
        elif number == 2:
            for d in peers:
                py_copy(d).wait_recv()
            summed = part_y[y_mine, :].astype(jnp.float32)
            for d in peers:
                summed += part_y_in[d - 1].astype(jnp.float32)
            part_z[z] = summed.astype(jnp.bfloat16)
            launch([pz_copy(d, z) for d in peers])
        elif number == 3:
            for d in peers:
                pz_copy(d, (z - d + SIDE) % SIDE).wait_recv()
            four = [part_z[n].astype(jnp.float32) for n in range(SIDE)]
            total_y[y_mine, :] = ((four[0] + four[1]) + (four[2] + four[3])).astype(jnp.bfloat16)
            launch([ty_copy(d, y) for d in peers])
        elif number == 4:
            for d in peers:
                ty_copy(d, (y - d + SIDE) % SIDE).wait_recv()
            for j in range(lanes):
                total[x_mine, j * 128:(j + 1) * 128] = total_y[j * x_rows:(j + 1) * x_rows, :]
            launch([tx_copy(d, m) for d in peers])
        elif number == 5:
            for d in peers:
                tx_copy(d, (m - d + SIDE) % SIDE).wait_recv()
            launch([tc_copy(mine)])
        elif number == 6:
            tc_copy(theirs).wait_recv()

    for task in order:
        if task[0] == "arrive":
            wait_half(*task[1:])
            launch([to_core(*task[1:])])
        elif task[0] == "send":
            launch([ring(*task[1:])])
        elif task[0] == "sweep":
            sweep(*task[1:])
        elif task[0] == "late":
            late(task[1])
        else:
            grad_step(task[1])

    if not is_first:
        out_ref[...] = out[...].astype(out_ref.dtype)
    for copy in sent:
        copy.wait_send()


def hop(is_first, slots, targets, count, lists, picks, agg, weight, grad, values, scale):
    rows, width = agg.shape
    slot_total, blk, _ = values.shape
    bf16, f32, i32 = jnp.bfloat16, jnp.float32, jnp.int32
    half_rows, x_rows = width // 2, width // 8
    lanes = width // 128
    y_rows = x_rows * lanes // SIDE
    vmem, smem = pl.BlockSpec(memory_space=pltpu.VMEM), pl.BlockSpec(memory_space=pltpu.SMEM)
    dma = pltpu.SemaphoreType.DMA
    peers = dma((SIDE - 1,))
    out_shape = [
        jax.ShapeDtypeStruct((rows, width), f32 if is_first else bf16),
        jax.ShapeDtypeStruct((width, width), bf16),
    ]
    out_specs = [vmem, vmem]
    scratch = [
        pltpu.VMEM((2, SIDE * SIDE, 2, blk, width), bf16),
        pltpu.VMEM((slot_total, blk, blk), bf16),
        pltpu.VMEM((2 * blk, blk), bf16),
        pltpu.VMEM((SIDE - 1, blk, width), bf16),
        pltpu.VMEM((2 + SIDE, blk, width), bf16),
        pltpu.VMEM((rows, width), bf16),
        pltpu.VMEM((width, width), f32),
        pltpu.VMEM((half_rows, width), f32),
        pltpu.VMEM((half_rows, width), bf16),
        pltpu.VMEM((SIDE - 1, x_rows, width), bf16),
        pltpu.VMEM((x_rows * lanes, 128), bf16),
        pltpu.VMEM((SIDE - 1, y_rows, 128), bf16),
        pltpu.VMEM((SIDE, y_rows, 128), bf16),
        pltpu.VMEM((x_rows * lanes, 128), bf16),
        dma(()),
        dma((SIDE * SIDE, 2, 2)), dma((SIDE * SIDE, 2, 2)),
        dma((SIDE * SIDE, 2, 2)), dma((SIDE * SIDE, 2, 2)),
        peers, peers, dma(()), dma(()),
        peers, peers, peers, peers, peers, peers, peers, peers, peers, peers, dma(()), dma(()),
    ]
    if is_first:
        out_shape.append(jax.ShapeDtypeStruct((2 * SIDE * SIDE,), i32))
        out_specs.append(smem)
        scratch += [
            pltpu.VMEM((SIDE, SIDE, 2, 8, 128), i32),
            pltpu.SMEM((SIDE, SIDE, 2, 1, 128), i32),
            dma(()), dma(()), dma(()), peers, peers, peers, peers,
        ]
    else:
        scratch.append(pltpu.VMEM((rows, width), f32))
    return pl.pallas_call(
        functools.partial(hop_kernel, scale, is_first),
        out_shape=tuple(out_shape),
        in_specs=[smem] * 4 + [vmem if is_first else smem] + [vmem] * 3 + [pl.BlockSpec(memory_space=pl.ANY)],
        out_specs=tuple(out_specs),
        scratch_shapes=scratch,
        compiler_params=pltpu.CompilerParams(
            collective_id=0 if is_first else 1, has_side_effects=True, vmem_limit_bytes=60 << 20
        ),
        name="hop_two" if is_first else "hop_one",
    )(slots, targets, count, lists, picks, agg, weight, grad, values)


def body(
    agg_one,
    agg_two,
    grad_out,
    hop_one_weight,
    hop_two_weight,
    block_values,
    src_slot,
    dst_block,
    block_count,
    send_member,
    send_group,
):
    total_labels = agg_one.shape[0] * lax.axis_size("member") * lax.axis_size("group")
    scale = float(total_labels) ** (-0.5)
    graph = (src_slot[0], dst_block[0], block_count, send_member[0, :, 0])
    carry, grad_w_two, picks = hop(
        True, *graph, send_group, agg_two, hop_two_weight, grad_out, block_values, scale
    )
    emb, grad_w_one = hop(
        False, *graph, picks, agg_one, hop_one_weight, carry, block_values, scale
    )
    return (emb, grad_w_one.astype(jnp.float32), grad_w_two.astype(jnp.float32))


def solution(mesh):
    in_specs = (
        P(("member", "group"), None),
        P(("member", "group"), None),
        P(("member", "group"), None),
        P(),
        P(),
        P(("member", "group"), None, None),
        P(("member", "group"), None),
        P(("member", "group"), None),
        P(("member", "group")),
        P(("member", "group"), None, None),
        P(("member", "group"), None),
    )
    out_specs = (P(("member", "group"), None), P(), P())
    return jax.shard_map(body, mesh=mesh, in_specs=in_specs, out_specs=out_specs, check_vma=False)
```

```python
import functools

import jax
import jax.numpy as jnp
from jax import lax
from jax.experimental import pallas as pl
from jax.experimental.pallas import tpu as pltpu
from jax.sharding import PartitionSpec as P

MESH = pl.DeviceIdType.MESH
SIDE = 4

STEP_US = {"arrive": 0.12, "sweep": 0.7, "late": 0.7, "grad": 1.0}
LINK_US = 2 * 0.1966 / 0.090
X_US = LINK_US
CORE_US = 0.1966 / 0.3
DELAY_US = 1.5
LATE_PARTS = 8
QUEUE_US = 4.8


def onward(dy, dz, b, part):
    first, second = (0, 1) if b == 0 else (1, 0)
    pos = (dy, dz)

    def step(axis, way):
        new = list(pos)
        new[axis] = (new[axis] + way) % SIDE
        return (new[0], new[1], b, part, axis, way)

    d1, d2 = pos[first], pos[second]
    moved = []
    if d2 == 0:
        if d1 == 0:
            moved += [step(first, 1), step(first, -1)]
        elif (d1, part) == (1, 0):
            moved.append(step(first, 1))
        elif (d1, part) == (3, 1):
            moved.append(step(first, -1))
        moved += [step(second, 1), step(second, -1)]
    elif (d2, part) == (1, 0):
        moved.append(step(second, 1))
    elif (d2, part) == (3, 1):
        moved.append(step(second, -1))
    return moved


def own_copies():
    early = [
        [(1, 0, 0, 0, 0, 1), (0, 1, 0, 0, 1, 1)],
        [(3, 0, 0, 1, 0, -1), (0, 3, 0, 1, 1, -1), (1, 0, 0, 1, 0, 1), (3, 0, 0, 0, 0, -1)],
        [(0, 1, 1, 0, 1, 1)],
        [(0, 3, 1, 1, 1, -1), (0, 1, 1, 1, 1, 1), (0, 3, 1, 0, 1, -1)],
    ]
    rest = [key for b in range(2) for part in range(2) for key in onward(0, 0, b, part)]
    for group in early:
        for key in group:
            rest.remove(key)
    return early, sorted(rest, key=lambda key: key[3] if key[5] == 1 else 1 - key[3])


def plan():
    free = {}
    here = {}

    def send(link, key, cost, now):
        start = max(free.get(link, 0.0), now)
        free[link] = start + cost
        here[key] = start + cost + DELAY_US

    held = []

    def flush():
        nonlocal now
        for key in sorted(held, key=lambda key: key[0] != 0 and key[1] != 0):
            if free.get(key[4:], 0.0) <= now + QUEUE_US:
                held.remove(key)
                result.append(("send",) + key)
                send(key[4:], ("ring",) + key[:4], LINK_US, now)
                waiting.add(key[:4])

    def send_core(key, now):
        send("core", ("core",) + key, CORE_US, now)

    def send_peers(axis, name, cost, now):
        send((axis, 1), (name, 1), cost, now)
        send((axis, -1), (name, 3), cost, now)
        send((axis, 1), (name, 2), 2 * cost, now)

    result, waiting = [], set()
    now = 6.0
    early, rest = own_copies()
    for number, group in enumerate(early):
        for key in group:
            send(key[4:], ("ring",) + key[:4], LINK_US, 1.5 + number)
            waiting.add(key[:4])
    held += rest
    for b in range(2):
        for part in range(2):
            send_core((0, 0, b, part), 3.0)
    send("core", ("pc", 0), 6 * CORE_US, 5.0)
    flush()
    seen = {(0, 0, b, part) for b in range(2) for part in range(2)}
    tasks = [("grad", n) for n in range(7)]
    tasks += [("sweep", 0, dy, dz) for dy in range(SIDE) for dz in range(SIDE) if (dy, dz) != (0, 0)]
    tasks += [("sweep", 1, dy, dz) for dy in range(SIDE) for dz in range(SIDE)]
    tasks += [("late", n) for n in range(LATE_PARTS)]
    needs = {0: ["pc"], 1: ["px"], 2: ["py"], 3: ["pz"], 4: ["ty"], 5: ["tx"], 6: ["tc"]}
    done_grad = -1

    def ready(task):
        if task[0] == "grad":
            if task[1] != done_grad + 1:
                return 1e9
            names = needs[task[1]]
            times = [here[key] for key in here if key[0] in names]
            return max(times)
        if task[0] == "late":
            times = [here[key] for key in here if key[0] == "member"]
            return max(times) if times else 1e9
        _, other, dy, dz = task
        keys = [(dy, dz, b, part) for b in range(2) for part in range(2)]
        if other == 0:
            return 0.0 if all(key in seen for key in keys) else 1e9
        return max(here.get(("core",) + key, 1e9) for key in keys)

    def price(task):
        if task[0] == "late":
            return STEP_US["late"] * 17 / LATE_PARTS
        return STEP_US[task[0]]

    def run(task):
        nonlocal now, done_grad
        now = max(now, ready(task)) + price(task)
        result.append(task)
        tasks.remove(task)
        if task[0] == "grad":
            done_grad = n = task[1]
            if n == 0:
                send_peers("x", "px", X_US * 0.75, now)
                send_peers("x", "member", 2 * X_US, now)
            elif n == 1:
                send_peers(0, "py", 0.1875 * LINK_US, now)
            elif n == 2:
                send_peers(1, "pz", 0.1875 * LINK_US, now)
            elif n == 3:
                send_peers(0, "ty", 0.1875 * LINK_US, now)
            elif n == 4:
                send_peers("x", "tx", X_US * 0.75, now)
            elif n == 5:
                send("core", ("tc", 0), 3 * CORE_US, now)

    while waiting or held:
        flush()
        coming = min(waiting, key=lambda key: (here[("ring",) + key], key))
        arrival = here[("ring",) + coming]
        if arrival > now:
            able = [task for task in tasks if ready(task) <= now]
            able = [task for task in able if now + price(task) <= arrival + 0.5]
            if able:
                run(able[0])
                flush()
                continue
            soon = [task for task in tasks if task[0] == "grad" and ready(task) + 0.2 <= arrival]
            if soon:
                run(soon[0])
                flush()
                continue
        now = max(now, arrival) + STEP_US["arrive"]
        waiting.remove(coming)
        seen.add(coming)
        result.append(("arrive",) + coming)
        held += onward(*coming)
        flush()
        send_core(coming, now)
    while tasks:
        run(min(tasks, key=lambda task: (ready(task), task[0])))
    return result, now


def slope(value):
    sig = jax.nn.sigmoid(value)
    return sig * (1.0 + value * (1.0 - sig))


def across(left, right, dims):
    return lax.dot_general(left, right, (dims, ((), ())), preferred_element_type=jnp.float32)


def hop_kernel(scale, is_first, *refs):
    (slots, targets, count, lists, picks_in, agg, weight, grad, values_hbm), refs = refs[:9], refs[9:]
    out_ref, total = refs[:2]
    refs = refs[2:]
    if is_first:
        picks_out, refs = refs[0], refs[1:]
    (
        pool, values, lhs, member_out, member_in, pull,
        part, part_core, part_x_out, part_x_in, part_y, part_y_in, part_z, total_y,
        values_sem, ring_send, ring_recv, core_send, core_recv, member_send, member_recv,
        pc_send, pc_recv, px_send, px_recv, py_send, py_recv, pz_send, pz_recv,
        ty_send, ty_recv, tx_send, tx_recv, tc_send, tc_recv,
    ), refs = refs[:35], refs[35:]
    if is_first:
        out = out_ref
        table, table_smem, picks_sem, kc_send, kc_recv, ky_send, ky_recv, kz_send, kz_recv = refs
        picks = picks_out
    else:
        (out,) = refs
        picks = picks_in
    blk = values.shape[1]
    width = weight.shape[0]
    slot_total = values.shape[0]
    half = blk // 2
    cut = min(256, width)
    m = lax.axis_index("member")
    g = lax.axis_index("group")
    y, z, c = g // (2 * SIDE), (g // 2) % SIDE, g % 2
    peers = range(1, SIDE)

    def at(dy, dz, other=0):
        core = c if other == 0 else 1 - c
        return (((y + dy) % SIDE) * SIDE + (z + dz) % SIDE) * 2 + core

    partner = {"group": at(0, 0, 1)}

    load_values = pltpu.make_async_copy(values_hbm, values, values_sem)
    load_values.start()

    barrier = pltpu.get_barrier_semaphore()
    for d in peers:
        for peer in ({"group": at(d, 0)}, {"group": at(0, d)}, {"member": (m + d) % SIDE}):
            pl.semaphore_signal(barrier, inc=1, device_id=peer, device_id_type=MESH)
    pl.semaphore_signal(barrier, inc=1, device_id=partner, device_id_type=MESH)

    def remote(src, dst, send, recv, peer):
        return pltpu.make_async_remote_copy(
            src_ref=src, dst_ref=dst, send_sem=send, recv_sem=recv, device_id=peer, device_id_type=MESH
        )

    sent = []

    def launch(copies):
        for copy in copies:
            copy.start()
            sent.append(copy)

    def ring(dy, dz, b, half_no, axis, way):
        rows = pl.ds(half_no * half, half)
        sdy, sdz = ((dy - way) % SIDE, dz) if axis == 0 else (dy, (dz - way) % SIDE)
        return remote(
            pool.at[0, sdy * SIDE + sdz, b, rows],
            pool.at[0, dy * SIDE + dz, b, rows],
            ring_send.at[dy * SIDE + dz, b, half_no],
            ring_recv.at[dy * SIDE + dz, b, half_no],
            {"group": at(way, 0) if axis == 0 else at(0, way)},
        )

    def wait_half(dy, dz, b, half_no):
        axis, d = (1, dz) if b == 0 else (0, dy)
        if d == 0:
            axis, d = (0, dy) if b == 0 else (1, dz)
        way = {1: 1, 3: -1, 2: 1 - 2 * half_no}[d]
        ring(dy, dz, b, half_no, axis, way).wait_recv()

    def to_core(dy, dz, b, half_no):
        rows = pl.ds(half_no * half, half)
        r = dy * SIDE + dz
        return remote(
            pool.at[0, r, b, rows], pool.at[1, r, b, rows],
            core_send.at[r, b, half_no], core_recv.at[r, b, half_no], partner,
        )

    if is_first:
        kc = remote(table.at[0, 0, 0], table.at[0, 0, 1], kc_send, kc_recv, partner)
        ky = [
            remote(table.at[0, 0], table.at[0, d], ky_send.at[d - 1], ky_recv.at[d - 1], {"group": at(d, 0)})
            for d in peers
        ]
        kz = [
            remote(table.at[0], table.at[d], kz_send.at[d - 1], kz_recv.at[d - 1], {"group": at(0, d)})
            for d in peers
        ]
        table[0, 0, 0] = jnp.zeros(table.shape[3:], jnp.int32)
        table[0, 0, 0, 0:1, 0:picks_in.shape[1]] = picks_in[...]

    early = own_copies()[0]

    def own_part(b, part_no):
        rows = pl.ds(b * blk + part_no * half, half)
        lift = across(agg[rows, :], weight[...], ((1,), (0,)))
        pulled = (grad[rows, :].astype(jnp.float32) * slope(lift)).astype(jnp.bfloat16)
        pull[rows, :] = pulled
        back = across(pulled, weight[...], ((1,), (1,))).astype(jnp.bfloat16)
        pool[0, 0, b, pl.ds(part_no * half, half), :] = back
        launch([ring(*key) for key in early[b * 2 + part_no]])

    pl.semaphore_wait(barrier, 3 * (SIDE - 1) + 1)
    if is_first:
        launch([kc])
    own_part(0, 0)
    if is_first:
        kc.wait_recv()
        launch(ky)
    own_part(0, 1)
    own_part(1, 0)
    if is_first:
        for copy in ky:
            copy.wait_recv()
        launch(kz)
    own_part(1, 1)
    order = plan()[0]
    while order[0][0] == "send":
        launch([ring(*order.pop(0)[1:])])
    launch([to_core(0, 0, b, part_no) for b in range(2) for part_no in range(2)])

    half_rows, x_rows = width // 2, width // 8
    lanes = width // 128
    y_rows = x_rows * lanes // SIDE

    @pl.loop(0, width // cut)
    def _(i):
        rows = pl.ds(pl.multiple_of(i * cut, cut), cut)
        part[rows, :] = across(agg[:, rows], pull[...], ((0,), (0,))) * scale

    mine = pl.ds(pl.multiple_of(c * half_rows, half_rows), half_rows)
    theirs = pl.ds(pl.multiple_of((1 - c) * half_rows, half_rows), half_rows)
    pc = remote(part.at[theirs], part_core, pc_send, pc_recv, partner)
    launch([pc])

    for d in peers:
        member_out[d - 1] = jnp.where(lists[(m + d) % SIDE] == 0, pool[0, 0, 0], pool[0, 0, 1])
    member_in[0] = pool[0, 0, 0]
    member_in[1] = pool[0, 0, 1]
    member_in[2 + m] = jnp.where(lists[m] == 0, pool[0, 0, 0], pool[0, 0, 1])
    out[...] = grad[...].astype(jnp.float32)
    load_values.wait()

    def member_copy(d, source):
        return remote(
            member_out.at[d - 1], member_in.at[2 + source], member_send.at[d - 1], member_recv.at[d - 1],
            {"member": (m + d) % SIDE},
        )

    def set_lhs(k, live):
        value = values[k].T
        zero = jnp.zeros_like(value)
        where = targets[k]
        lhs[0:blk, :] = jnp.where(jnp.logical_and(live, where == 0), value, zero)
        lhs[blk:2 * blk, :] = jnp.where(jnp.logical_and(live, where == 1), value, zero)

    def take_picks():
        for copy in kz:
            copy.wait_recv()
        fetch = pltpu.make_async_copy(table.at[:, :, :, pl.ds(0, 1)], table_smem, picks_sem)
        fetch.start()
        fetch.wait()
        for other in range(2):
            for dy in range(SIDE):
                for dz in range(SIDE):
                    picks_out[other * SIDE * SIDE + dy * SIDE + dz] = table_smem[dz, dy, other, 0, g]

    picks_here = [not is_first]

    def sweep(other, dy, dz):
        if not picks_here[0]:
            take_picks()
            picks_here[0] = True
        if other == 1:
            for b in range(2):
                for part_no in range(2):
                    to_core(dy, dz, b, part_no).wait_recv()
        groups = 2 * SIDE * SIDE
        r = dy * SIDE + dz
        set_lhs((at(-dy, -dz, other) - g - 1 + groups) % groups, True)
        pick = picks[other * SIDE * SIDE + r]

        for n in range(width // cut):
            cols = pl.ds(n * cut, cut)
            block = jnp.where(pick == 0, pool[other, r, 0, :, cols], pool[other, r, 1, :, cols])
            out[:, cols] += across(lhs[...], block, ((1,), (0,)))

    def late(number):
        start = 2 * SIDE * SIDE - 1
        total_late = slot_total - start
        if number == 0:
            for d in peers:
                member_copy(d, (m - d + SIDE) % SIDE).wait_recv()

        @pl.loop(start + total_late * number // LATE_PARTS, start + total_late * (number + 1) // LATE_PARTS)
        def _(k):
            set_lhs(k, k < count[0])

            for n in range(width // cut):
                cols = pl.ds(n * cut, cut)
                out[:, cols] += across(lhs[...], member_in[slots[k], :, cols], ((1,), (0,)))

    def px_copy(d):
        rows = pl.ds(pl.multiple_of(((m + d) % SIDE) * x_rows, x_rows), x_rows)
        return remote(
            part_x_out.at[rows], part_x_in.at[d - 1], px_send.at[d - 1], px_recv.at[d - 1],
            {"member": (m + d) % SIDE},
        )

    def py_copy(d):
        rows = pl.ds(pl.multiple_of(((y + d) % SIDE) * y_rows, y_rows), y_rows)
        return remote(
            part_y.at[rows], part_y_in.at[d - 1], py_send.at[d - 1], py_recv.at[d - 1],
            {"group": at(d, 0)},
        )

    def pz_copy(d, place):
        return remote(
            part_z.at[z], part_z.at[place], pz_send.at[d - 1], pz_recv.at[d - 1], {"group": at(0, d)}
        )

    def ty_copy(d, place):
        rows = pl.ds(pl.multiple_of(y * y_rows, y_rows), y_rows)
        there = pl.ds(pl.multiple_of(place * y_rows, y_rows), y_rows)
        return remote(
            total_y.at[rows], total_y.at[there], ty_send.at[d - 1], ty_recv.at[d - 1], {"group": at(d, 0)}
        )

    def tx_copy(d, place):
        rows = pl.ds(pl.multiple_of(c * half_rows + m * x_rows, x_rows), x_rows)
        there = pl.ds(pl.multiple_of(c * half_rows + place * x_rows, x_rows), x_rows)
        return remote(
            total.at[rows], total.at[there], tx_send.at[d - 1], tx_recv.at[d - 1],
            {"member": (m + d) % SIDE},
        )

    def tc_copy(there):
        return remote(total.at[mine], total.at[there], tc_send, tc_recv, partner)

    x_mine = pl.ds(pl.multiple_of(c * half_rows + m * x_rows, x_rows), x_rows)
    y_mine = pl.ds(pl.multiple_of(y * y_rows, y_rows), y_rows)

    def grad_step(number):
        if number == 0:
            pc.wait_recv()
            part[mine, :] += part_core[...]
            part_x_out[...] = part[mine, :].astype(jnp.bfloat16)
            launch([px_copy(d) for d in peers])
            launch([member_copy(d, m) for d in peers])
        elif number == 1:
            for d in peers:
                px_copy(d).wait_recv()
            summed = part[x_mine, :]
            for d in peers:
                summed += part_x_in[d - 1].astype(jnp.float32)
            for j in range(lanes):
                part_y[j * x_rows:(j + 1) * x_rows, :] = summed[:, j * 128:(j + 1) * 128].astype(jnp.bfloat16)
            launch([py_copy(d) for d in peers])
        elif number == 2:
            for d in peers:
                py_copy(d).wait_recv()
            summed = part_y[y_mine, :].astype(jnp.float32)
            for d in peers:
                summed += part_y_in[d - 1].astype(jnp.float32)
            part_z[z] = summed.astype(jnp.bfloat16)
            launch([pz_copy(d, z) for d in peers])
        elif number == 3:
            for d in peers:
                pz_copy(d, (z - d + SIDE) % SIDE).wait_recv()
            four = [part_z[n].astype(jnp.float32) for n in range(SIDE)]
            total_y[y_mine, :] = ((four[0] + four[1]) + (four[2] + four[3])).astype(jnp.bfloat16)
            launch([ty_copy(d, y) for d in peers])
        elif number == 4:
            for d in peers:
                ty_copy(d, (y - d + SIDE) % SIDE).wait_recv()
            for j in range(lanes):
                total[x_mine, j * 128:(j + 1) * 128] = total_y[j * x_rows:(j + 1) * x_rows, :]
            launch([tx_copy(d, m) for d in peers])
        elif number == 5:
            for d in peers:
                tx_copy(d, (m - d + SIDE) % SIDE).wait_recv()
            launch([tc_copy(mine)])
        elif number == 6:
            tc_copy(theirs).wait_recv()

    for task in order:
        if task[0] == "arrive":
            wait_half(*task[1:])
            launch([to_core(*task[1:])])
        elif task[0] == "send":
            launch([ring(*task[1:])])
        elif task[0] == "sweep":
            sweep(*task[1:])
        elif task[0] == "late":
            late(task[1])
        else:
            grad_step(task[1])

    if not is_first:
        out_ref[...] = out[...].astype(out_ref.dtype)
    for copy in sent:
        copy.wait_send()


def hop(is_first, slots, targets, count, lists, picks, agg, weight, grad, values, scale):
    rows, width = agg.shape
    slot_total, blk, _ = values.shape
    bf16, f32, i32 = jnp.bfloat16, jnp.float32, jnp.int32
    half_rows, x_rows = width // 2, width // 8
    lanes = width // 128
    y_rows = x_rows * lanes // SIDE
    vmem, smem = pl.BlockSpec(memory_space=pltpu.VMEM), pl.BlockSpec(memory_space=pltpu.SMEM)
    dma = pltpu.SemaphoreType.DMA
    peers = dma((SIDE - 1,))
    out_shape = [
        jax.ShapeDtypeStruct((rows, width), f32 if is_first else bf16),
        jax.ShapeDtypeStruct((width, width), bf16),
    ]
    out_specs = [vmem, vmem]
    scratch = [
        pltpu.VMEM((2, SIDE * SIDE, 2, blk, width), bf16),
        pltpu.VMEM((slot_total, blk, blk), bf16),
        pltpu.VMEM((2 * blk, blk), bf16),
        pltpu.VMEM((SIDE - 1, blk, width), bf16),
        pltpu.VMEM((2 + SIDE, blk, width), bf16),
        pltpu.VMEM((rows, width), bf16),
        pltpu.VMEM((width, width), f32),
        pltpu.VMEM((half_rows, width), f32),
        pltpu.VMEM((half_rows, width), bf16),
        pltpu.VMEM((SIDE - 1, x_rows, width), bf16),
        pltpu.VMEM((x_rows * lanes, 128), bf16),
        pltpu.VMEM((SIDE - 1, y_rows, 128), bf16),
        pltpu.VMEM((SIDE, y_rows, 128), bf16),
        pltpu.VMEM((x_rows * lanes, 128), bf16),
        dma(()),
        dma((SIDE * SIDE, 2, 2)), dma((SIDE * SIDE, 2, 2)),
        dma((SIDE * SIDE, 2, 2)), dma((SIDE * SIDE, 2, 2)),
        peers, peers, dma(()), dma(()),
        peers, peers, peers, peers, peers, peers, peers, peers, peers, peers, dma(()), dma(()),
    ]
    if is_first:
        out_shape.append(jax.ShapeDtypeStruct((2 * SIDE * SIDE,), i32))
        out_specs.append(smem)
        scratch += [
            pltpu.VMEM((SIDE, SIDE, 2, 8, 128), i32),
            pltpu.SMEM((SIDE, SIDE, 2, 1, 128), i32),
            dma(()), dma(()), dma(()), peers, peers, peers, peers,
        ]
    else:
        scratch.append(pltpu.VMEM((rows, width), f32))
    return pl.pallas_call(
        functools.partial(hop_kernel, scale, is_first),
        out_shape=tuple(out_shape),
        in_specs=[smem] * 4 + [vmem if is_first else smem] + [vmem] * 3 + [pl.BlockSpec(memory_space=pl.ANY)],
        out_specs=tuple(out_specs),
        scratch_shapes=scratch,
        compiler_params=pltpu.CompilerParams(
            collective_id=0 if is_first else 1, has_side_effects=True, vmem_limit_bytes=60 << 20
        ),
        name="hop_two" if is_first else "hop_one",
    )(slots, targets, count, lists, picks, agg, weight, grad, values)


def finish_kernel(emb, one, two, emb_out, one_out, two_out):
    emb_out[...] = emb[...]
    one_out[...] = one[...].astype(jnp.float32)
    two_out[...] = two[...].astype(jnp.float32)


def finish(emb, one, two):
    steps = 2
    specs = [pl.BlockSpec((array.shape[0] // steps, array.shape[1]), lambda i: (i, 0)) for array in (emb, one, two)]
    return pl.pallas_call(
        finish_kernel,
        grid=(steps,),
        out_shape=(
            jax.ShapeDtypeStruct(emb.shape, emb.dtype),
            jax.ShapeDtypeStruct(one.shape, jnp.float32),
            jax.ShapeDtypeStruct(two.shape, jnp.float32),
        ),
        in_specs=specs,
        out_specs=tuple(specs),
        name="finish",
    )(emb, one, two)


def body(
    agg_one,
    agg_two,
    grad_out,
    hop_one_weight,
    hop_two_weight,
    block_values,
    src_slot,
    dst_block,
    block_count,
    send_member,
    send_group,
):
    total_labels = agg_one.shape[0] * lax.axis_size("member") * lax.axis_size("group")
    scale = float(total_labels) ** (-0.5)
    graph = (src_slot[0], dst_block[0], block_count, send_member[0, :, 0])
    carry, grad_w_two, picks = hop(
        True, *graph, send_group, agg_two, hop_two_weight, grad_out, block_values, scale
    )
    emb, grad_w_one = hop(
        False, *graph, picks, agg_one, hop_one_weight, carry, block_values, scale
    )
    return finish(emb, grad_w_one, grad_w_two)


def solution(mesh):
    in_specs = (
        P(("member", "group"), None),
        P(("member", "group"), None),
        P(("member", "group"), None),
        P(),
        P(),
        P(("member", "group"), None, None),
        P(("member", "group"), None),
        P(("member", "group"), None),
        P(("member", "group")),
        P(("member", "group"), None, None),
        P(("member", "group"), None),
    )
    out_specs = (P(("member", "group"), None), P(), P())
    return jax.shard_map(body, mesh=mesh, in_specs=in_specs, out_specs=out_specs, check_vma=False)
```

```python
import functools

import jax
import jax.numpy as jnp
from jax import lax
from jax.experimental import pallas as pl
from jax.experimental.pallas import tpu as pltpu
from jax.sharding import PartitionSpec as P

MESH = pl.DeviceIdType.MESH
SIDE = 4

STEP_US = {"arrive": 0.12, "sweep": 0.7, "late": 0.7, "grad": 1.0}
LINK_US = 2 * 0.1966 / 0.090
X_US = LINK_US
CORE_US = 0.1966 / 0.3
DELAY_US = 1.5
LATE_PARTS = 8
QUEUE_US = 4.8


def onward(dy, dz, b, part):
    first, second = (0, 1) if b == 0 else (1, 0)
    pos = (dy, dz)

    def step(axis, way):
        new = list(pos)
        new[axis] = (new[axis] + way) % SIDE
        return (new[0], new[1], b, part, axis, way)

    d1, d2 = pos[first], pos[second]
    moved = []
    if d2 == 0:
        if d1 == 0:
            moved += [step(first, 1), step(first, -1)]
        elif (d1, part) == (1, 0):
            moved.append(step(first, 1))
        elif (d1, part) == (3, 1):
            moved.append(step(first, -1))
        moved += [step(second, 1), step(second, -1)]
    elif (d2, part) == (1, 0):
        moved.append(step(second, 1))
    elif (d2, part) == (3, 1):
        moved.append(step(second, -1))
    return moved


def own_copies():
    early = [
        [(1, 0, 0, 0, 0, 1), (0, 1, 0, 0, 1, 1)],
        [(3, 0, 0, 1, 0, -1), (0, 3, 0, 1, 1, -1), (1, 0, 0, 1, 0, 1), (3, 0, 0, 0, 0, -1)],
        [(0, 1, 1, 0, 1, 1)],
        [(0, 3, 1, 1, 1, -1), (0, 1, 1, 1, 1, 1), (0, 3, 1, 0, 1, -1)],
    ]
    rest = [key for b in range(2) for part in range(2) for key in onward(0, 0, b, part)]
    for group in early:
        for key in group:
            rest.remove(key)
    return early, sorted(rest, key=lambda key: key[3] if key[5] == 1 else 1 - key[3])


def plan():
    free = {}
    here = {}

    def send(link, key, cost, now):
        start = max(free.get(link, 0.0), now)
        free[link] = start + cost
        here[key] = start + cost + DELAY_US

    held = []

    def flush():
        nonlocal now
        for key in sorted(held, key=lambda key: key[0] != 0 and key[1] != 0):
            if free.get(key[4:], 0.0) <= now + QUEUE_US:
                held.remove(key)
                result.append(("send",) + key)
                send(key[4:], ("ring",) + key[:4], LINK_US, now)
                waiting.add(key[:4])

    def send_core(key, now):
        send("core", ("core",) + key, CORE_US, now)

    def send_peers(axis, name, cost, now):
        send((axis, 1), (name, 1), cost, now)
        send((axis, -1), (name, 3), cost, now)
        send((axis, 1), (name, 2), 2 * cost, now)

    result, waiting = [], set()
    now = 6.0
    early, rest = own_copies()
    for number, group in enumerate(early):
        for key in group:
            send(key[4:], ("ring",) + key[:4], LINK_US, 1.5 + number)
            waiting.add(key[:4])
    held += rest
    for b in range(2):
        for part in range(2):
            send_core((0, 0, b, part), 3.0)
    send("core", ("pc", 0), 6 * CORE_US, 5.0)
    flush()
    seen = {(0, 0, b, part) for b in range(2) for part in range(2)}
    tasks = [("grad", n) for n in range(7)]
    tasks += [("sweep", 0, dy, dz) for dy in range(SIDE) for dz in range(SIDE) if (dy, dz) != (0, 0)]
    tasks += [("sweep", 1, dy, dz) for dy in range(SIDE) for dz in range(SIDE)]
    tasks += [("late", n) for n in range(LATE_PARTS)]
    needs = {0: ["pc"], 1: ["px"], 2: ["py"], 3: ["pz"], 4: ["ty"], 5: ["tx"], 6: ["tc"]}
    done_grad = -1

    def ready(task):
        if task[0] == "grad":
            if task[1] != done_grad + 1:
                return 1e9
            names = needs[task[1]]
            times = [here[key] for key in here if key[0] in names]
            return max(times)
        if task[0] == "late":
            times = [here[key] for key in here if key[0] == "member"]
            return max(times) if times else 1e9
        _, other, dy, dz = task
        keys = [(dy, dz, b, part) for b in range(2) for part in range(2)]
        if other == 0:
            return 0.0 if all(key in seen for key in keys) else 1e9
        return max(here.get(("core",) + key, 1e9) for key in keys)

    def price(task):
        if task[0] == "late":
            return STEP_US["late"] * 17 / LATE_PARTS
        return STEP_US[task[0]]

    def run(task):
        nonlocal now, done_grad
        now = max(now, ready(task)) + price(task)
        result.append(task)
        tasks.remove(task)
        if task[0] == "grad":
            done_grad = n = task[1]
            if n == 0:
                send_peers("x", "px", X_US * 0.75, now)
                send_peers("x", "member", 2 * X_US, now)
            elif n == 1:
                send_peers(0, "py", 0.1875 * LINK_US, now)
            elif n == 2:
                send_peers(1, "pz", 0.1875 * LINK_US, now)
            elif n == 3:
                send_peers(0, "ty", 0.1875 * LINK_US, now)
            elif n == 4:
                send_peers("x", "tx", X_US * 0.75, now)
            elif n == 5:
                send("core", ("tc", 0), 3 * CORE_US, now)

    while waiting or held:
        flush()
        coming = min(waiting, key=lambda key: (here[("ring",) + key], key))
        arrival = here[("ring",) + coming]
        if arrival > now:
            able = [task for task in tasks if ready(task) <= now]
            able = [task for task in able if now + price(task) <= arrival + 0.1]
            if able:
                run(able[0])
                flush()
                continue
            soon = [task for task in tasks if task[0] == "grad" and ready(task) + 0.2 <= arrival]
            if soon:
                run(soon[0])
                flush()
                continue
        now = max(now, arrival) + STEP_US["arrive"]
        waiting.remove(coming)
        seen.add(coming)
        result.append(("arrive",) + coming)
        held += onward(*coming)
        flush()
        send_core(coming, now)
    while tasks:
        run(min(tasks, key=lambda task: (ready(task), task[0])))
    return result, now


def slope(value):
    sig = jax.nn.sigmoid(value)
    return sig * (1.0 + value * (1.0 - sig))


def across(left, right, dims):
    return lax.dot_general(left, right, (dims, ((), ())), preferred_element_type=jnp.float32)


def hop_kernel(scale, is_first, *refs):
    (slots, targets, count, lists, picks_in, agg, weight, grad, values_hbm), refs = refs[:9], refs[9:]
    out_ref, total = refs[:2]
    refs = refs[2:]
    if is_first:
        picks_out, refs = refs[0], refs[1:]
    (
        pool, values, lhs, member_out, member_in, pull,
        part, part_core, part_x_out, part_x_in, part_y, part_y_in, part_z, total_y,
        values_sem, ring_send, ring_recv, core_send, core_recv, member_send, member_recv,
        pc_send, pc_recv, px_send, px_recv, py_send, py_recv, pz_send, pz_recv,
        ty_send, ty_recv, tx_send, tx_recv, tc_send, tc_recv,
    ), refs = refs[:35], refs[35:]
    if is_first:
        out = out_ref
        table, table_smem, picks_sem, kc_send, kc_recv, ky_send, ky_recv, kz_send, kz_recv = refs
        picks = picks_out
    else:
        (out,) = refs
        picks = picks_in
    blk = values.shape[1]
    width = weight.shape[0]
    slot_total = values.shape[0]
    half = blk // 2
    cut = min(256, width)
    m = lax.axis_index("member")
    g = lax.axis_index("group")
    y, z, c = g // (2 * SIDE), (g // 2) % SIDE, g % 2
    peers = range(1, SIDE)

    def at(dy, dz, other=0):
        core = c if other == 0 else 1 - c
        return (((y + dy) % SIDE) * SIDE + (z + dz) % SIDE) * 2 + core

    partner = {"group": at(0, 0, 1)}

    load_values = pltpu.make_async_copy(values_hbm, values, values_sem)
    load_values.start()

    barrier = pltpu.get_barrier_semaphore()
    for d in peers:
        for peer in ({"group": at(d, 0)}, {"group": at(0, d)}, {"member": (m + d) % SIDE}):
            pl.semaphore_signal(barrier, inc=1, device_id=peer, device_id_type=MESH)
    pl.semaphore_signal(barrier, inc=1, device_id=partner, device_id_type=MESH)

    def remote(src, dst, send, recv, peer):
        return pltpu.make_async_remote_copy(
            src_ref=src, dst_ref=dst, send_sem=send, recv_sem=recv, device_id=peer, device_id_type=MESH
        )

    sent = []

    def launch(copies):
        for copy in copies:
            copy.start()
            sent.append(copy)

    def ring(dy, dz, b, half_no, axis, way):
        rows = pl.ds(half_no * half, half)
        sdy, sdz = ((dy - way) % SIDE, dz) if axis == 0 else (dy, (dz - way) % SIDE)
        return remote(
            pool.at[0, sdy * SIDE + sdz, b, rows],
            pool.at[0, dy * SIDE + dz, b, rows],
            ring_send.at[dy * SIDE + dz, b, half_no],
            ring_recv.at[dy * SIDE + dz, b, half_no],
            {"group": at(way, 0) if axis == 0 else at(0, way)},
        )

    def wait_half(dy, dz, b, half_no):
        axis, d = (1, dz) if b == 0 else (0, dy)
        if d == 0:
            axis, d = (0, dy) if b == 0 else (1, dz)
        way = {1: 1, 3: -1, 2: 1 - 2 * half_no}[d]
        ring(dy, dz, b, half_no, axis, way).wait_recv()

    def to_core(dy, dz, b, half_no):
        rows = pl.ds(half_no * half, half)
        r = dy * SIDE + dz
        return remote(
            pool.at[0, r, b, rows], pool.at[1, r, b, rows],
            core_send.at[r, b, half_no], core_recv.at[r, b, half_no], partner,
        )

    if is_first:
        kc = remote(table.at[0, 0, 0], table.at[0, 0, 1], kc_send, kc_recv, partner)
        ky = [
            remote(table.at[0, 0], table.at[0, d], ky_send.at[d - 1], ky_recv.at[d - 1], {"group": at(d, 0)})
            for d in peers
        ]
        kz = [
            remote(table.at[0], table.at[d], kz_send.at[d - 1], kz_recv.at[d - 1], {"group": at(0, d)})
            for d in peers
        ]
        table[0, 0, 0] = jnp.zeros(table.shape[3:], jnp.int32)
        table[0, 0, 0, 0:1, 0:picks_in.shape[1]] = picks_in[...]

    early = own_copies()[0]

    def own_part(b, part_no):
        rows = pl.ds(b * blk + part_no * half, half)
        lift = across(agg[rows, :], weight[...], ((1,), (0,)))
        pulled = (grad[rows, :].astype(jnp.float32) * slope(lift)).astype(jnp.bfloat16)
        pull[rows, :] = pulled
        back = across(pulled, weight[...], ((1,), (1,))).astype(jnp.bfloat16)
        pool[0, 0, b, pl.ds(part_no * half, half), :] = back
        launch([ring(*key) for key in early[b * 2 + part_no]])

    pl.semaphore_wait(barrier, 3 * (SIDE - 1) + 1)
    if is_first:
        launch([kc])
    own_part(0, 0)
    if is_first:
        kc.wait_recv()
        launch(ky)
    own_part(0, 1)
    own_part(1, 0)
    if is_first:
        for copy in ky:
            copy.wait_recv()
        launch(kz)
    own_part(1, 1)
    order = plan()[0]
    while order[0][0] == "send":
        launch([ring(*order.pop(0)[1:])])
    launch([to_core(0, 0, b, part_no) for b in range(2) for part_no in range(2)])

    half_rows, x_rows = width // 2, width // 8
    lanes = width // 128
    y_rows = x_rows * lanes // SIDE

    @pl.loop(0, width // cut)
    def _(i):
        rows = pl.ds(pl.multiple_of(i * cut, cut), cut)
        part[rows, :] = across(agg[:, rows], pull[...], ((0,), (0,))) * scale

    mine = pl.ds(pl.multiple_of(c * half_rows, half_rows), half_rows)
    theirs = pl.ds(pl.multiple_of((1 - c) * half_rows, half_rows), half_rows)
    pc = remote(part.at[theirs], part_core, pc_send, pc_recv, partner)
    launch([pc])

    for d in peers:
        member_out[d - 1] = jnp.where(lists[(m + d) % SIDE] == 0, pool[0, 0, 0], pool[0, 0, 1])
    member_in[0] = pool[0, 0, 0]
    member_in[1] = pool[0, 0, 1]
    member_in[2 + m] = jnp.where(lists[m] == 0, pool[0, 0, 0], pool[0, 0, 1])
    out[...] = grad[...].astype(jnp.float32)
    load_values.wait()

    def member_copy(d, source):
        return remote(
            member_out.at[d - 1], member_in.at[2 + source], member_send.at[d - 1], member_recv.at[d - 1],
            {"member": (m + d) % SIDE},
        )

    def set_lhs(k, live):
        value = values[k].T
        zero = jnp.zeros_like(value)
        where = targets[k]
        lhs[0:blk, :] = jnp.where(jnp.logical_and(live, where == 0), value, zero)
        lhs[blk:2 * blk, :] = jnp.where(jnp.logical_and(live, where == 1), value, zero)

    def take_picks():
        for copy in kz:
            copy.wait_recv()
        fetch = pltpu.make_async_copy(table.at[:, :, :, pl.ds(0, 1)], table_smem, picks_sem)
        fetch.start()
        fetch.wait()
        for other in range(2):
            for dy in range(SIDE):
                for dz in range(SIDE):
                    picks_out[other * SIDE * SIDE + dy * SIDE + dz] = table_smem[dz, dy, other, 0, g]

    picks_here = [not is_first]

    def sweep(other, dy, dz):
        if not picks_here[0]:
            take_picks()
            picks_here[0] = True
        if other == 1:
            for b in range(2):
                for part_no in range(2):
                    to_core(dy, dz, b, part_no).wait_recv()
        groups = 2 * SIDE * SIDE
        r = dy * SIDE + dz
        set_lhs((at(-dy, -dz, other) - g - 1 + groups) % groups, True)
        pick = picks[other * SIDE * SIDE + r]

        for n in range(width // cut):
            cols = pl.ds(n * cut, cut)
            block = jnp.where(pick == 0, pool[other, r, 0, :, cols], pool[other, r, 1, :, cols])
            out[:, cols] += across(lhs[...], block, ((1,), (0,)))

    def late(number):
        start = 2 * SIDE * SIDE - 1
        total_late = slot_total - start
        if number == 0:
            for d in peers:
                member_copy(d, (m - d + SIDE) % SIDE).wait_recv()

        @pl.loop(start + total_late * number // LATE_PARTS, start + total_late * (number + 1) // LATE_PARTS)
        def _(k):
            set_lhs(k, k < count[0])

            for n in range(width // cut):
                cols = pl.ds(n * cut, cut)
                out[:, cols] += across(lhs[...], member_in[slots[k], :, cols], ((1,), (0,)))

    def px_copy(d):
        rows = pl.ds(pl.multiple_of(((m + d) % SIDE) * x_rows, x_rows), x_rows)
        return remote(
            part_x_out.at[rows], part_x_in.at[d - 1], px_send.at[d - 1], px_recv.at[d - 1],
            {"member": (m + d) % SIDE},
        )

    def py_copy(d):
        rows = pl.ds(pl.multiple_of(((y + d) % SIDE) * y_rows, y_rows), y_rows)
        return remote(
            part_y.at[rows], part_y_in.at[d - 1], py_send.at[d - 1], py_recv.at[d - 1],
            {"group": at(d, 0)},
        )

    def pz_copy(d, place):
        return remote(
            part_z.at[z], part_z.at[place], pz_send.at[d - 1], pz_recv.at[d - 1], {"group": at(0, d)}
        )

    def ty_copy(d, place):
        rows = pl.ds(pl.multiple_of(y * y_rows, y_rows), y_rows)
        there = pl.ds(pl.multiple_of(place * y_rows, y_rows), y_rows)
        return remote(
            total_y.at[rows], total_y.at[there], ty_send.at[d - 1], ty_recv.at[d - 1], {"group": at(d, 0)}
        )

    def tx_copy(d, place):
        rows = pl.ds(pl.multiple_of(c * half_rows + m * x_rows, x_rows), x_rows)
        there = pl.ds(pl.multiple_of(c * half_rows + place * x_rows, x_rows), x_rows)
        return remote(
            total.at[rows], total.at[there], tx_send.at[d - 1], tx_recv.at[d - 1],
            {"member": (m + d) % SIDE},
        )

    def tc_copy(there):
        return remote(total.at[mine], total.at[there], tc_send, tc_recv, partner)

    x_mine = pl.ds(pl.multiple_of(c * half_rows + m * x_rows, x_rows), x_rows)
    y_mine = pl.ds(pl.multiple_of(y * y_rows, y_rows), y_rows)

    def grad_step(number):
        if number == 0:
            pc.wait_recv()
            part[mine, :] += part_core[...]
            part_x_out[...] = part[mine, :].astype(jnp.bfloat16)
            launch([px_copy(d) for d in peers])
            launch([member_copy(d, m) for d in peers])
        elif number == 1:
            for d in peers:
                px_copy(d).wait_recv()
            summed = part[x_mine, :]
            for d in peers:
                summed += part_x_in[d - 1].astype(jnp.float32)
            for j in range(lanes):
                part_y[j * x_rows:(j + 1) * x_rows, :] = summed[:, j * 128:(j + 1) * 128].astype(jnp.bfloat16)
            launch([py_copy(d) for d in peers])
        elif number == 2:
            for d in peers:
                py_copy(d).wait_recv()
            summed = part_y[y_mine, :].astype(jnp.float32)
            for d in peers:
                summed += part_y_in[d - 1].astype(jnp.float32)
            part_z[z] = summed.astype(jnp.bfloat16)
            launch([pz_copy(d, z) for d in peers])
        elif number == 3:
            for d in peers:
                pz_copy(d, (z - d + SIDE) % SIDE).wait_recv()
            four = [part_z[n].astype(jnp.float32) for n in range(SIDE)]
            total_y[y_mine, :] = ((four[0] + four[1]) + (four[2] + four[3])).astype(jnp.bfloat16)
            launch([ty_copy(d, y) for d in peers])
        elif number == 4:
            for d in peers:
                ty_copy(d, (y - d + SIDE) % SIDE).wait_recv()
            for j in range(lanes):
                total[x_mine, j * 128:(j + 1) * 128] = total_y[j * x_rows:(j + 1) * x_rows, :]
            launch([tx_copy(d, m) for d in peers])
        elif number == 5:
            for d in peers:
                tx_copy(d, (m - d + SIDE) % SIDE).wait_recv()
            launch([tc_copy(mine)])
        elif number == 6:
            tc_copy(theirs).wait_recv()

    for task in order:
        if task[0] == "arrive":
            wait_half(*task[1:])
            launch([to_core(*task[1:])])
        elif task[0] == "send":
            launch([ring(*task[1:])])
        elif task[0] == "sweep":
            sweep(*task[1:])
        elif task[0] == "late":
            late(task[1])
        else:
            grad_step(task[1])

    if not is_first:
        out_ref[...] = out[...].astype(out_ref.dtype)
    for copy in sent:
        copy.wait_send()


def hop(is_first, slots, targets, count, lists, picks, agg, weight, grad, values, scale):
    rows, width = agg.shape
    slot_total, blk, _ = values.shape
    bf16, f32, i32 = jnp.bfloat16, jnp.float32, jnp.int32
    half_rows, x_rows = width // 2, width // 8
    lanes = width // 128
    y_rows = x_rows * lanes // SIDE
    vmem, smem = pl.BlockSpec(memory_space=pltpu.VMEM), pl.BlockSpec(memory_space=pltpu.SMEM)
    dma = pltpu.SemaphoreType.DMA
    peers = dma((SIDE - 1,))
    out_shape = [
        jax.ShapeDtypeStruct((rows, width), f32 if is_first else bf16),
        jax.ShapeDtypeStruct((width, width), bf16),
    ]
    out_specs = [vmem, vmem]
    scratch = [
        pltpu.VMEM((2, SIDE * SIDE, 2, blk, width), bf16),
        pltpu.VMEM((slot_total, blk, blk), bf16),
        pltpu.VMEM((2 * blk, blk), bf16),
        pltpu.VMEM((SIDE - 1, blk, width), bf16),
        pltpu.VMEM((2 + SIDE, blk, width), bf16),
        pltpu.VMEM((rows, width), bf16),
        pltpu.VMEM((width, width), f32),
        pltpu.VMEM((half_rows, width), f32),
        pltpu.VMEM((half_rows, width), bf16),
        pltpu.VMEM((SIDE - 1, x_rows, width), bf16),
        pltpu.VMEM((x_rows * lanes, 128), bf16),
        pltpu.VMEM((SIDE - 1, y_rows, 128), bf16),
        pltpu.VMEM((SIDE, y_rows, 128), bf16),
        pltpu.VMEM((x_rows * lanes, 128), bf16),
        dma(()),
        dma((SIDE * SIDE, 2, 2)), dma((SIDE * SIDE, 2, 2)),
        dma((SIDE * SIDE, 2, 2)), dma((SIDE * SIDE, 2, 2)),
        peers, peers, dma(()), dma(()),
        peers, peers, peers, peers, peers, peers, peers, peers, peers, peers, dma(()), dma(()),
    ]
    if is_first:
        out_shape.append(jax.ShapeDtypeStruct((2 * SIDE * SIDE,), i32))
        out_specs.append(smem)
        scratch += [
            pltpu.VMEM((SIDE, SIDE, 2, 8, 128), i32),
            pltpu.SMEM((SIDE, SIDE, 2, 1, 128), i32),
            dma(()), dma(()), dma(()), peers, peers, peers, peers,
        ]
    else:
        scratch.append(pltpu.VMEM((rows, width), f32))
    return pl.pallas_call(
        functools.partial(hop_kernel, scale, is_first),
        out_shape=tuple(out_shape),
        in_specs=[smem] * 4 + [vmem if is_first else smem] + [vmem] * 3 + [pl.BlockSpec(memory_space=pl.ANY)],
        out_specs=tuple(out_specs),
        scratch_shapes=scratch,
        compiler_params=pltpu.CompilerParams(
            collective_id=0 if is_first else 1, has_side_effects=True, vmem_limit_bytes=60 << 20
        ),
        name="hop_two" if is_first else "hop_one",
    )(slots, targets, count, lists, picks, agg, weight, grad, values)


def finish_kernel(emb, one, two, emb_out, one_out, two_out):
    emb_out[...] = emb[...]
    one_out[...] = one[...].astype(jnp.float32)
    two_out[...] = two[...].astype(jnp.float32)


def finish(emb, one, two):
    steps = 2
    specs = [pl.BlockSpec((array.shape[0] // steps, array.shape[1]), lambda i: (i, 0)) for array in (emb, one, two)]
    return pl.pallas_call(
        finish_kernel,
        grid=(steps,),
        out_shape=(
            jax.ShapeDtypeStruct(emb.shape, emb.dtype),
            jax.ShapeDtypeStruct(one.shape, jnp.float32),
            jax.ShapeDtypeStruct(two.shape, jnp.float32),
        ),
        in_specs=specs,
        out_specs=tuple(specs),
        name="finish",
    )(emb, one, two)


def body(
    agg_one,
    agg_two,
    grad_out,
    hop_one_weight,
    hop_two_weight,
    block_values,
    src_slot,
    dst_block,
    block_count,
    send_member,
    send_group,
):
    total_labels = agg_one.shape[0] * lax.axis_size("member") * lax.axis_size("group")
    scale = float(total_labels) ** (-0.5)
    graph = (src_slot[0], dst_block[0], block_count, send_member[0, :, 0])
    carry, grad_w_two, picks = hop(
        True, *graph, send_group, agg_two, hop_two_weight, grad_out, block_values, scale
    )
    emb, grad_w_one = hop(
        False, *graph, picks, agg_one, hop_one_weight, carry, block_values, scale
    )
    return finish(emb, grad_w_one, grad_w_two)


def solution(mesh):
    in_specs = (
        P(("member", "group"), None),
        P(("member", "group"), None),
        P(("member", "group"), None),
        P(),
        P(),
        P(("member", "group"), None, None),
        P(("member", "group"), None),
        P(("member", "group"), None),
        P(("member", "group")),
        P(("member", "group"), None, None),
        P(("member", "group"), None),
    )
    out_specs = (P(("member", "group"), None), P(), P())
    return jax.shard_map(body, mesh=mesh, in_specs=in_specs, out_specs=out_specs, check_vma=False)
```
